512 devices in a mesh: dp: 16 (over x, y_hi, core), tensor: 32 (over z, y_lo).
Axes of the slice: x: 4, y: 8 (y_hi: 2, y_lo: 4; y = y_hi * 4 + y_lo), z: 8, core: 2. Of those that a mesh axis runs over, the one named last changes fastest.
Arguments:
- token_ids: int32 [4, 640], P(None, 'dp'), may hold values from 0 to 81919
- lengths: int32 [640], P('dp'), may hold values from 2 to 64, as said below
- embed_table: bfloat16 [16, 32, 16, 81920], P(None, 'tensor', 'dp')
- norm_gain: bfloat16 [8192], P('tensor'), may hold values from 0.5 to 1.5
- w_query: bfloat16 [8192, 8192], P('dp', 'tensor'), may hold values from -0.0625 to 0.0625
- key_value_weight: bfloat16 [8192, 2048], P('dp', 'tensor'), may hold values from -0.0625 to 0.0625
- w_out: bfloat16 [8192, 8192], P('tensor', 'dp'), may hold values from -0.125 to 0.125
- key_value_cache: bfloat16 [640, 32, 16, 256], P('dp', 'tensor'), as said below
Outputs:
- hidden: bfloat16 [4, 640, 8192], P(None, 'dp', 'tensor')
The draws below stay inside these ranges and needn't reach their ends.
Inputs may be any that keep to these rules, and one draw needn't show every extreme that they name: `lengths`: some row has exactly 64 cached positions. `key_value_cache`: keys are stored already rotated for their positions.
All inputs are finite; a program needn't handle non-finite values.
Results may differ from the reference program's by a relative error of at most 0.024.
Values may be sent and summed in bfloat16 or wider, within the bound.
A program may use at most 128 MiB of HBM per device.

```python
import math
import jax
import jax.numpy as jnp
import numpy as np
from jax import lax

MODEL_WIDTH = 8192
QUERY_HEADS = 64
KEY_HEADS = 8
HEAD_SIZE = 128
V = 81920
DECODE_STEPS = 4
CACHE_SLOTS = 64
DECODED_ROWS = 640
TENSOR_SHARE = 4
BLOCK_POSITIONS = 16
FD = 16
N_DP = 16
N_TENSOR = 32


def draw_lengths(key, part):
    key = jax.random.fold_in(key, 31)
    first_key, spot_key = jax.random.split(key)
    drawn = jax.random.randint(first_key, (DECODED_ROWS,), 2, CACHE_SLOTS + 1)
    spot = jax.random.randint(spot_key, (), 0, DECODED_ROWS)
    return jnp.where(jnp.arange(DECODED_ROWS) == spot, CACHE_SLOTS, drawn).astype(jnp.int32)


def draw_embed_table(key, part):
    key = jax.random.fold_in(key, 11)
    feat_key, token_key, base_key = jax.random.split(key, 3)
    feature_scale = jnp.exp(jax.random.uniform(feat_key, (FD, N_TENSOR, N_DP, 1), minval=0.0, maxval=2.3026))
    token_scale = jnp.exp(jax.random.uniform(token_key, (1, 1, 1, V), minval=0.0, maxval=2.3026))
    base = jax.random.normal(base_key, (FD, N_TENSOR, N_DP, V))
    return (0.02 * base * feature_scale * token_scale).astype(jnp.bfloat16)


def draw_key_value_cache(key, part):
    key = jax.random.fold_in(key, 23)
    base_key = jax.random.fold_in(key, 0)
    array_shape = (DECODED_ROWS, KEY_HEADS, TENSOR_SHARE, BLOCK_POSITIONS, 2 * HEAD_SIZE)
    complete_rows = jax.random.normal(base_key, array_shape)
    return complete_rows.reshape(DECODED_ROWS, KEY_HEADS * TENSOR_SHARE, BLOCK_POSITIONS, 2 * HEAD_SIZE).astype(jnp.bfloat16)


def set_ends(result, rng, low, top_value):
    shape = result.shape
    spot = [jax.random.randint(jax.random.fold_in(rng, axis), (), 0, shape[axis]) for axis in range(len(shape))]
    result = result.at[tuple(spot)].set(low)
    longest = shape.index(max(shape))
    spot[longest] = (spot[longest] + 1) % shape[longest]
    return result.at[tuple(spot)].set(top_value)


def with_spikes(values, stream_key, source, target, shards_of, factor):
    def block_of(dim):
        return (jnp.arange(values.shape[dim]) // (values.shape[dim] // shards_of)).reshape((-1,) + (1,) * (values.ndim - 1 - dim))

    one_side = jax.random.permutation(stream_key, shards_of)[block_of(target)]
    second = (block_of(target) + shards_of // 2) % shards_of
    return jnp.where((block_of(source) == one_side) | (block_of(source) == second), factor * values, values)


def block_scale(stream_key, dims, cuts, least, top_value):
    def one(position, shards_of):
        steps = jax.random.uniform(jax.random.fold_in(jax.random.fold_in(stream_key, 6), position), (shards_of,), jnp.float32, least / len(cuts), top_value / len(cuts))
        return jnp.repeat(jnp.exp(steps), dims[position] // shards_of).reshape((-1,) + (1,) * (len(dims) - position - 1))

    loudness = one(*cuts[0])
    for cut in cuts[1:]:
        loudness = loudness * one(*cut)
    return loudness


def skewed_wide(rng, shape, count, slope):
    loads = [min(1 << octave, count + 1 - (1 << octave)) * (1 << 20) // math.isqrt((1 << octave) ** slope) + 1 for octave in range((count + 1).bit_length()) if 1 << octave <= count]
    width = 1 + sum(loads) // (1 << 30)
    listing = np.cumsum(np.array([max(1, weight // width) for weight in loads]))
    ticket = jax.random.randint(jax.random.fold_in(rng, 1), shape, 0, int(listing[len(loads) - 1]))
    start = jnp.left_shift(1, jnp.searchsorted(jnp.asarray(listing, jnp.int32), ticket, side="right").astype(jnp.int32))
    rank = start - 1 + jax.random.randint(jax.random.fold_in(rng, 4), shape, 0, 1 << 30) % jnp.minimum(start, count + 1 - start)
    return jax.random.permutation(jax.random.fold_in(rng, 2), count)[rank].astype(jnp.int32)


def normal_values(own_key, shape, width, most, pieces=(), held_as=jnp.bfloat16):
    entries = jax.random.normal(own_key, shape, jnp.float32) * width
    if len(pieces) > 0:
        entries = block_scale(own_key, shape, pieces, -0.22, 0.18) * entries
    return jnp.clip(entries, min=-most, max=most).astype(held_as)


def noise_with(key, shape, width, reach, cuts, heavy, held_as=jnp.bfloat16):
    values = width * jax.random.normal(key, shape, jnp.float32)
    if cuts:
        values = values * block_scale(key, shape, cuts, -0.22, 0.18)
    return jnp.clip(with_spikes(values, jax.random.fold_in(key, 3), *heavy), -reach, reach).astype(held_as)


def setup_inputs(seed: int = 0) -> dict:
    seeds = jax.random.split(jax.random.key(seed), 9)
    return {
        "token_ids": set_ends(skewed_wide(seeds[0], (DECODE_STEPS, DECODED_ROWS), V, 2), jax.random.fold_in(seeds[0], 3), 0, V - 1).astype(jnp.int32),
        "lengths": draw_lengths(jax.random.fold_in(seeds[8], 71), 0),
        "embed_table": draw_embed_table(jax.random.fold_in(seeds[8], 71), 0),
        "norm_gain": jnp.clip(1.0 + 0.1 * jax.random.normal(seeds[3], (MODEL_WIDTH,), jnp.float32), 0.5, 1.5).astype(jnp.bfloat16),
        "w_query": normal_values(seeds[4], (MODEL_WIDTH, QUERY_HEADS * HEAD_SIZE), MODEL_WIDTH ** -0.5, 0.0625, ((0, 16), (1, 32))),
        "key_value_weight": normal_values(seeds[5], (MODEL_WIDTH, 2 * KEY_HEADS * HEAD_SIZE), MODEL_WIDTH ** -0.5, 0.0625, ((0, 16), (1, 32))),
        "w_out": noise_with(seeds[6], (QUERY_HEADS * HEAD_SIZE, MODEL_WIDTH), (QUERY_HEADS * HEAD_SIZE) ** -0.5, 0.125, ((0, 32), (1, 16)), (0, 1, 32, 2.75)),
        "key_value_cache": draw_key_value_cache(jax.random.fold_in(seeds[8], 71), 0),
    }


EPS = 1e-06
THETA = 1000000.0

def rotate(vectors, turn):
    half_width = vectors.shape[-1] // 2
    front_half = vectors[..., :half_width]
    back_half = vectors[..., half_width:]
    cosine = jnp.cos(turn)
    sine_part = jnp.sin(turn)
    return jnp.concatenate([front_half * cosine - back_half * sine_part, back_half * cosine + front_half * sine_part], axis=-1)

def angles(positions, half_width):
    frequency = THETA ** (-(jnp.arange(half_width, dtype=jnp.float32) / half_width))
    return positions.astype(jnp.float32)[..., None] * frequency

def reference(token_ids, lengths, embed_table, norm_gain, w_query, key_value_weight, w_out, key_value_cache):
    looked = jnp.take(embed_table, token_ids.reshape(-1), axis=3)
    embedded = jnp.transpose(looked, (3, 1, 2, 0)).reshape(DECODE_STEPS, DECODED_ROWS, MODEL_WIDTH)
    embed_f = embedded.astype(jnp.float32)
    factor = lax.rsqrt(lax.optimization_barrier(jnp.mean(embed_f * embed_f, axis=-1, keepdims=True)) + EPS)
    normed = (embed_f * factor * norm_gain.astype(jnp.float32)).astype(jnp.bfloat16)
    flat_rows = normed.reshape(DECODE_STEPS * DECODED_ROWS, MODEL_WIDTH)
    positions = lengths[None, :].astype(jnp.int32) + jnp.arange(DECODE_STEPS, dtype=jnp.int32)[:, None]
    turn = angles(positions, HEAD_SIZE // 2)
    query_raw = jnp.dot(flat_rows, w_query, preferred_element_type=jnp.float32).reshape(DECODE_STEPS, DECODED_ROWS, QUERY_HEADS, HEAD_SIZE)
    query_rows = rotate(query_raw, turn[:, :, None, :]).astype(jnp.bfloat16)
    key_value_rows = jnp.dot(flat_rows, key_value_weight, preferred_element_type=jnp.float32).astype(jnp.bfloat16)
    key_value_rows = key_value_rows.reshape(DECODE_STEPS, DECODED_ROWS, KEY_HEADS, 2, HEAD_SIZE)
    key_new = rotate(key_value_rows[:, :, :, 0, :].astype(jnp.float32), turn[:, :, None, :]).astype(jnp.bfloat16)
    value_new = key_value_rows[:, :, :, 1, :]
    cache_gathered = key_value_cache.reshape(DECODED_ROWS, KEY_HEADS, CACHE_SLOTS, 2 * HEAD_SIZE)
    cache_keys = cache_gathered[..., :HEAD_SIZE].astype(jnp.float32)
    cache_vals = cache_gathered[..., HEAD_SIZE:].astype(jnp.float32)
    query_groups = QUERY_HEADS // KEY_HEADS
    query_grouped = query_rows.astype(jnp.float32).reshape(DECODE_STEPS, DECODED_ROWS, KEY_HEADS, query_groups, HEAD_SIZE)
    inv_root = 1.0 / math.sqrt(HEAD_SIZE)
    scores_old = jnp.einsum('srhgd,rhcd->srhgc', query_grouped, cache_keys) * inv_root
    scores_new = jnp.einsum('srhgd,trhd->srhgt', query_grouped, key_new.astype(jnp.float32)) * inv_root
    valid_old = jnp.arange(CACHE_SLOTS, dtype=jnp.int32)[None, None, None, None, :] < lengths.astype(jnp.int32)[None, :, None, None, None]
    valid_new = jnp.arange(DECODE_STEPS, dtype=jnp.int32)[None, None, None, None, :] <= jnp.arange(DECODE_STEPS, dtype=jnp.int32)[:, None, None, None, None]
    scores_old = jnp.where(valid_old, scores_old, -1e+30)
    scores_new = jnp.where(valid_new, scores_new, -1e+30)
    top_score = jnp.maximum(lax.optimization_barrier(jnp.max(scores_old, axis=-1, keepdims=True)), lax.optimization_barrier(jnp.max(scores_new, axis=-1, keepdims=True)))
    exp_old = jnp.exp(scores_old - top_score)
    exp_new = jnp.exp(scores_new - top_score)
    totals = lax.optimization_barrier(jnp.sum(exp_old, axis=-1, keepdims=True)) + lax.optimization_barrier(jnp.sum(exp_new, axis=-1, keepdims=True))
    probs_old = (exp_old / totals).astype(jnp.bfloat16).astype(jnp.float32)
    probs_new = (exp_new / totals).astype(jnp.bfloat16).astype(jnp.float32)
    attended = jnp.einsum('srhgc,rhcd->srhgd', probs_old, cache_vals)
    attended = attended + jnp.einsum('srhgt,trhd->srhgd', probs_new, value_new.astype(jnp.float32))
    attended = attended.astype(jnp.bfloat16).reshape(DECODE_STEPS * DECODED_ROWS, N_TENSOR, QUERY_HEADS * HEAD_SIZE // N_TENSOR)
    weight_groups = w_out.reshape(N_TENSOR, QUERY_HEADS * HEAD_SIZE // N_TENSOR, MODEL_WIDTH)

    def add_group(running, pair):
        term = jnp.dot(pair[0], pair[1], preferred_element_type=jnp.float32).astype(jnp.bfloat16)
        term = lax.optimization_barrier(term)
        return (running + term.astype(jnp.float32), None)
    summed, unused = lax.scan(add_group, jnp.zeros((DECODE_STEPS * DECODED_ROWS, MODEL_WIDTH), jnp.float32), (jnp.moveaxis(attended, 1, 0), weight_groups))
    return (embed_f + summed.reshape(DECODE_STEPS, DECODED_ROWS, MODEL_WIDTH)).astype(jnp.bfloat16)
```

```python
import functools
import math

import jax
import jax.numpy as jnp
from jax import lax
from jax.experimental import pallas as pl
from jax.experimental.pallas import tpu as pltpu
from jax.sharding import PartitionSpec as P

EPS = 1e-06
THETA = 1000000.0
BF = jnp.bfloat16
F32 = jnp.float32

NX = 4
NZ = 8
NB = 4
QROWS = 40
QPAD = 48
NROWS = 160
XROWS = 176
HEAD = 128
FULL = 8192

MESH = pl.DeviceIdType.MESH


def exchange_tokens(tok_ref, all_ref, send_sem, recv_sem):
    dp = lax.axis_index("dp")
    barrier = pltpu.get_barrier_semaphore()
    for i in range(1, 16):
        pl.semaphore_signal(
            barrier, inc=1, device_id={"dp": (dp + i) % 16}, device_id_type=MESH
        )
    pl.semaphore_wait(barrier, 15)
    copies = []
    for i in range(1, 16):
        copy = pltpu.make_async_remote_copy(
            src_ref=tok_ref,
            dst_ref=all_ref.at[dp],
            send_sem=send_sem.at[i],
            recv_sem=recv_sem,
            device_id={"dp": (dp + i) % 16},
            device_id_type=MESH,
        )
        copy.start()
        copies.append(copy)
    pltpu.make_async_copy(tok_ref, all_ref.at[dp], recv_sem).start()
    pltpu.make_async_copy(all_ref, all_ref, recv_sem).wait()
    for copy in copies:
        copy.wait_send()


def look_up(toks, table_ref, gain_ref, found_ref):
    lane = lax.broadcasted_iota(jnp.int32, (16, 128), 1)
    gain_tail = jnp.where(lane == NROWS - 128, gain_ref[...], 0.0)

    def entry(e, carry):
        for s in (0, 1):
            d2 = ((e // 2) * 2 + s) * 2 + e % 2
            for half, count in ((0, 128), (1, NROWS - 128)):

                def one(n, held):
                    token = toks[d2, half, n]
                    block = lax.shift_right_logical(token, 7)
                    offset = jnp.bitwise_and(token, 127)
                    tile = table_ref[:, pl.ds(pl.multiple_of(block * 128, 128), 128)]
                    turned = pltpu.roll(
                        tile.astype(F32), jnp.bitwise_and(n + 128 - offset, 127), 1
                    )
                    return jnp.where(lane == n, turned, held)

                start = jnp.zeros((16, 128), F32) if half == 0 else gain_tail
                found = lax.fori_loop(0, count, one, start, unroll=16)
                found_ref[e, s, :, pl.ds(half * 128, 128)] = found.astype(BF)
        return carry

    lax.fori_loop(0, 8, entry, 0)


def kernel(
    found_ref,
    ws_ref,
    wo_ref,
    cache_ref,
    cos_ref,
    sin_ref,
    len_ref,
    out_ref,
    lrecv,
    xt,
    xb,
    res,
    wbuf,
    wobuf,
    cbuf,
    qsend,
    qrecv,
    asend,
    arecv,
    att,
    qacc,
    kvacc,
    ssq,
    acc,
    sbuf,
    rright,
    rleft,
    frecv,
    send_sem,
    l_sem,
    x_sem,
    res_sem,
    w_sem,
    wo_sem,
    c_sem,
    q_sem,
    a_sem,
    rr_sem,
    rl_sem,
    f_sem,
):
    dp = lax.axis_index("dp")
    tn = lax.axis_index("tensor")
    x = dp // 4
    yh = (dp // 2) % 2
    c = dp % 2
    z = tn // 4
    b = tn % 4
    zpar = z % 2
    match = zpar == yh
    pair = b // 2
    bset = b % 2

    def dev(dp_, tn_):
        return {"dp": dp_, "tensor": tn_}

    def dpi(x_, yh_, c_):
        return (x_ * 2 + yh_) * 2 + c_

    pending = []
    counter = [0]

    def remote(src, dst, rsem, where, cond=None):
        n = counter[0]
        counter[0] += 1
        copy = pltpu.make_async_remote_copy(
            src_ref=src,
            dst_ref=dst,
            send_sem=send_sem.at[n],
            recv_sem=rsem,
            device_id=where,
            device_id_type=MESH,
        )
        if cond is None:
            copy.start()
        else:
            pl.when(cond)(copy.start)
        pending.append((cond, copy))

    def local(src, dst, sem, cond=None):
        copy = pltpu.make_async_copy(src, dst, sem)
        if cond is None:
            copy.start()
        else:
            pl.when(cond)(copy.start)

    def arrived(dst, sem):
        pltpu.make_async_copy(dst, dst, sem).wait()

    def to(src, dst, rsem, dp_, tn_):
        here = jnp.logical_and(dp_ == dp, tn_ == tn)
        remote(src, dst, rsem, dev(dp_, tn_), jnp.logical_not(here))
        local(src, dst, rsem, here)

    xr = (x + 1) % NX
    xl = (x + NX - 1) % NX
    xo = (x + 2) % NX
    zr = (z + 1) % NZ
    zl = (z + NZ - 1) % NZ
    right_z = dev(dp, zr * NB + b)
    left_z = dev(dp, zl * NB + b)

    barrier = pltpu.get_barrier_semaphore()
    partners = 0
    for i in range(1, 16):
        pl.semaphore_signal(barrier, inc=1, device_id=dev((dp + i) % 16, tn), device_id_type=MESH)
        partners += 1
    for i in range(1, 8):
        if i == 4:
            continue
        u = (yh * 4 + b + i) % 8
        pl.semaphore_signal(
            barrier, inc=1, device_id=dev(dpi(x, u // 4, c), z * NB + u % 4), device_id_type=MESH
        )
        partners += 1
    for where in (right_z, left_z):
        pl.semaphore_signal(barrier, inc=1, device_id=where, device_id_type=MESH)
        partners += 1
    pl.semaphore_wait(barrier, partners)

    for e in range(8):
        to(found_ref.at[e], lrecv.at[dp], l_sem, dpi(e // 2, zpar, e % 2), tn)

    class Gather:
        def __init__(self, src, buf, sem, half):
            self.src, self.buf, self.sem, self.half = src, buf, sem, half

        def slot(self, q, x_, c_, h=None):
            ref = self.buf.at[q, x_, c_]
            if h is None:
                return ref
            return ref.at[pl.ds(h * self.half, self.half)]

        def s(self, q, x_, c_, h=0):
            return self.sem.at[((q * NX + x_) * 2 + c_) * 2 + h]

        def send(self, src, q, x_, where):
            remote(src, self.slot(q, x_, c), self.s(q, x_, c), where)

        def first(self):
            own = (bset, x)
            local(self.src, self.slot(*own, c), self.s(*own, c))
            self.send(self.src, *own, dev(dp, z * NB + pair * 2 + 1 - bset))
            self.send(self.src, *own, dev(dpi(xr, yh, c), tn))
            self.send(self.src, *own, dev(dpi(xl, yh, c), tn))
            self.send(self.src, *own, dev(dpi(x, yh, 1 - c), tn))

        def second(self):
            q = 1 - bset
            arrived(self.slot(q, x, c), self.s(q, x, c))
            src = self.slot(q, x, c)
            self.send(src, q, x, dev(dpi(xr, yh, c), tn))
            self.send(src, q, x, dev(dpi(xl, yh, c), tn))
            self.send(src, q, x, dev(dpi(x, yh, 1 - c), tn))

        def relay(self, q):
            for x_, h, to_x in ((xl, 0, xr), (xr, 1, xl)):
                arrived(self.slot(q, x_, c), self.s(q, x_, c))
                remote(
                    self.slot(q, x_, c, h),
                    self.slot(q, x_, c, h),
                    self.s(q, x_, c, h),
                    dev(dpi(to_x, yh, c), tn),
                )
                self.send(self.slot(q, x_, c), q, x_, dev(dpi(x, yh, 1 - c), tn))

        def last(self, q):
            for h in (0, 1):
                arrived(self.slot(q, xo, c, h), self.s(q, xo, c, h))
            self.send(self.slot(q, xo, c), q, xo, dev(dpi(x, yh, 1 - c), tn))

        def finish(self):
            arrived(self.slot(bset, x, c), self.s(bset, x, c))
            for q in (0, 1):
                for x_ in range(NX):
                    arrived(self.slot(q, x_, 1 - c), self.s(q, x_, 1 - c))

    wqkv = Gather(ws_ref, wbuf, w_sem, 320)
    wout = Gather(wo_ref, wobuf, wo_sem, 128)
    wqkv.first()

    for i in range(NB):
        b2 = (b + i) % NB
        to(cache_ref.at[pl.ds(b2 * 10, 10)], cbuf.at[b], c_sem, dp, z * NB + b2)

    wqkv.second()
    wqkv.relay(bset)

    k_here = z // 2

    @pl.when(match)
    def _():
        arrived(lrecv, l_sem)
        for s in (0, 1):
            features = lrecv[:, s].reshape(256, 256).astype(F32)
            xt[s] = features.T[:XROWS].astype(BF)

    for s in (0, 1):
        for h in (0, 1):
            b2 = s + 2 * h
            same = b2 == b
            remote(
                xt.at[s],
                xb.at[k_here, b],
                x_sem.at[k_here * NB + b],
                dev(dp, z * NB + b2),
                jnp.logical_and(match, jnp.logical_not(same)),
            )
            local(
                xt.at[s], xb.at[k_here, b], x_sem.at[k_here * NB + b], jnp.logical_and(match, same)
            )

    def gather_z(j):
        delta = jnp.where(match, (0, 2, 6, 4)[j], (1, 7, 3, 5)[j])
        k = ((z - delta + NZ) % NZ) // 2
        for b_ in range(NB):
            reach = 4 if b_ < 2 else 3
            block = xb.at[k, b_]
            sem = x_sem.at[k * NB + b_]
            arrived(block, sem)
            if j < 3:
                remote(block, block, sem, right_z, delta < reach)
                remote(
                    block,
                    block,
                    sem,
                    left_z,
                    jnp.logical_or(
                        delta == 0, jnp.logical_and(delta > reach, 8 - delta < 7 - reach)
                    ),
                )
            else:
                remote(block, block, sem, right_z, delta < reach)
                remote(
                    block,
                    block,
                    sem,
                    left_z,
                    jnp.logical_and(delta > reach, 8 - delta < 7 - reach),
                )
        return k

    def project(k, start):
        for b_ in range(NB):
            raw = xb[k, b_].astype(F32)
            rows = raw[:NROWS]
            gain = raw[NROWS : NROWS + 1]
            scaled = (rows * gain).astype(BF)
            square = rows * rows
            square = square[:, :128] + square[:, 128:]
            c_ = b_ // 2
            h = b_ % 2
            parts = [
                jnp.dot(
                    scaled, wbuf[q, k, c_, h * 256 : h * 256 + 256], preferred_element_type=F32
                )
                for q in (0, 1)
            ]
            keyval = jnp.concatenate(
                [wbuf[q, k, c_, 512 + h * 64 : 576 + h * 64] for q in (0, 1)], axis=0
            )
            kv = lax.dot_general(
                scaled, keyval, (((1,), (1,)), ((), ())), preferred_element_type=F32
            )
            if start and b_ == 0:
                ssq[...] = square
                qacc[:, :256] = parts[0]
                qacc[:, 256:] = parts[1]
                kvacc[...] = kv
            else:
                ssq[...] += square
                qacc[:, :256] += parts[0]
                qacc[:, 256:] += parts[1]
                kvacc[...] += kv

    ks = [gather_z(0)]
    wqkv.relay(1 - bset)
    ks.append(gather_z(1))
    wqkv.last(bset)
    wqkv.last(1 - bset)
    wout.first()
    wqkv.finish()
    project(ks[0], True)
    ks.append(gather_z(2))
    project(ks[1], False)
    project(ks[2], False)
    ks.append(gather_z(3))
    project(ks[3], False)

    for_partner = 1 - zpar
    remote(xt.at[for_partner], res, res_sem, dev(dpi(x, for_partner, c), tn), match)
    local(xt.at[yh], res, res_sem, match)

    row40 = lax.broadcasted_iota(jnp.int32, (QROWS, 128), 0)
    lane40 = lax.broadcasted_iota(jnp.int32, (QROWS, 128), 1)
    diagonal = row40 == lane40
    row8 = lax.broadcasted_iota(jnp.int32, (8, 128), 0)
    for i in range(NB):
        total = jnp.sum(ssq[i * QROWS : (i + 1) * QROWS], axis=1, keepdims=True)
        flat = jnp.sum(jnp.where(diagonal, total, 0.0), axis=0, keepdims=True)
        high = flat.astype(BF).astype(F32)
        low = flat - high
        tail = jnp.where(row8 == 0, high, jnp.where(row8 == 1, low, 0.0))
        tail = jnp.concatenate([tail, jnp.zeros((8, 512), F32)], axis=1)
        body_rows = jnp.concatenate(
            [qacc[i * QROWS : (i + 1) * QROWS], kvacc[i * QROWS : (i + 1) * QROWS]], axis=1
        )
        qsend[i] = jnp.concatenate([body_rows, tail], axis=0).astype(BF)
        to(
            qsend.at[i],
            qrecv.at[yh, pair],
            q_sem.at[yh * 2 + pair],
            dpi(x, bset, c),
            z * NB + i,
        )

    wout.second()
    wout.relay(bset)

    for i in range(NB):
        arrived(qrecv.at[i // 2, i % 2], q_sem.at[i])
    arrived(cbuf, c_sem)

    tails = qrecv[0, 0, 32:QPAD, :128].astype(F32) + qrecv[1, 0, 32:QPAD, :128].astype(F32)
    flat = tails[8:9] + tails[9:10]
    total = jnp.sum(jnp.where(diagonal, flat, 0.0), axis=1, keepdims=True)
    factor = lax.rsqrt(total * (1.0 / FULL) + EPS)
    cosine = cos_ref[...]
    sine = sin_ref[...]

    def rope(u):
        return u * cosine + pltpu.roll(u, HEAD // 2, 1) * sine

    heads = []
    news = []
    for p in (0, 1):
        both = qrecv[0, p].astype(F32) + qrecv[1, p].astype(F32)
        both = both[:QROWS] * factor
        for i in range(4):
            heads.append(rope(both[:, i * HEAD : (i + 1) * HEAD]))
        news.append(both[:, 512:640])
    query = jnp.concatenate(heads, axis=0).astype(BF)
    no_rows = jnp.zeros((128 - QROWS, HEAD), F32)
    key_new = rope(news[0].astype(BF).astype(F32))
    key_new = jnp.concatenate([key_new, no_rows], axis=0).astype(BF)
    value_new = jnp.concatenate([news[1], no_rows], axis=0).astype(BF)
    keys = cbuf[:, :, :, :HEAD].reshape(640, HEAD)
    values = cbuf[:, :, :, HEAD:].reshape(640, HEAD)

    contract_last = (((1,), (1,)), ((), ()))
    inv_root = 1.0 / math.sqrt(HEAD)
    scores_old = lax.dot_general(query, keys, contract_last, preferred_element_type=F32) * inv_root
    scores_new = (
        lax.dot_general(query, key_new, contract_last, preferred_element_type=F32) * inv_root
    )
    col = lax.broadcasted_iota(jnp.int32, (QROWS, 640), 1)
    row = lax.broadcasted_iota(jnp.int32, (QROWS, 640), 0) // 4
    within = col % 160
    position = (col // 160) * 16 + within % 16
    old_ok = jnp.logical_and(within // 16 == row, position < len_ref[:, :1])
    new_ok = jnp.logical_and(
        lane40 // 4 == row40 // 4, jnp.logical_and(lane40 <= row40, lane40 < QROWS)
    )
    old_bias = jnp.where(old_ok, 0.0, -1e30)
    new_bias = jnp.where(new_ok, 0.0, -1e30)
    old_bias = jnp.concatenate([old_bias] * 8, axis=0)
    new_bias = jnp.concatenate([new_bias] * 8, axis=0)
    scores_old = jnp.where(old_bias == 0.0, scores_old, -1e30)
    scores_new = jnp.where(new_bias == 0.0, scores_new, -1e30)
    top = jnp.maximum(
        jnp.max(scores_old, axis=1, keepdims=True), jnp.max(scores_new, axis=1, keepdims=True)
    )
    exp_old = jnp.exp(scores_old - top)
    exp_new = jnp.exp(scores_new - top)
    totals = jnp.sum(exp_old, axis=1, keepdims=True) + jnp.sum(exp_new, axis=1, keepdims=True)
    probs_old = (exp_old / totals).astype(BF)
    probs_new = (exp_new / totals).astype(BF)
    attended = jnp.dot(probs_old, values, preferred_element_type=F32)
    attended = attended + jnp.dot(probs_new, value_new, preferred_element_type=F32)
    for p in (0, 1):
        side = jnp.concatenate(
            [attended[(4 * p + i) * QROWS : (4 * p + i + 1) * QROWS] for i in range(4)], axis=1
        )
        asend[p] = jnp.concatenate([side, jnp.zeros((QPAD - QROWS, 512), F32)], axis=0).astype(BF)
        for y_ in (0, 1):
            to(asend.at[p], arecv.at[b], a_sem.at[b], dpi(x, y_, c), z * NB + p * 2 + yh)

    wout.relay(1 - bset)
    wout.last(bset)
    wout.last(1 - bset)
    wout.finish()
    for i in range(NB):
        arrived(arecv.at[i], a_sem.at[i])
    att[...] = jnp.concatenate(
        [arecv[i].astype(F32)[:QROWS] for i in range(NB)], axis=0
    ).astype(BF)

    for j in range(4):
        delta = jnp.where(match, (4, 2, 6, 0)[j], (3, 5, 1, 7)[j])
        k = ((z + delta) % NZ) // 2
        is_end = delta == 0
        for b_ in range(NB):
            reach = 4 if b_ < 2 else 3
            c_ = b_ // 2
            h = b_ % 2
            part = jnp.dot(
                att[:, :256],
                wobuf[0, k, c_, :, h * 256 : h * 256 + 256],
                preferred_element_type=F32,
            )
            part = part + jnp.dot(
                att[:, 256:],
                wobuf[1, k, c_, :, h * 256 : h * 256 + 256],
                preferred_element_type=F32,
            )
            acc[...] = part
            go_right = jnp.logical_and(delta >= 1, delta <= reach)
            go_left = delta > reach
            from_left = delta + 1 <= reach
            from_right = jnp.logical_or(delta > reach + 1, is_end)
            index = k * NB + b_

            @pl.when(from_left)
            def _(index=index, k=k, b_=b_):
                arrived(rright.at[k, b_], rr_sem.at[index])
                acc[...] += rright[k, b_].astype(F32)

            @pl.when(from_right)
            def _(index=index, k=k, b_=b_):
                arrived(rleft.at[k, b_], rl_sem.at[index])
                acc[...] += rleft[k, b_].astype(F32)

            sbuf[k, b_] = acc[...].astype(BF)
            remote(sbuf.at[k, b_], rright.at[k, b_], rr_sem.at[index], right_z, go_right)
            remote(sbuf.at[k, b_], rleft.at[k, b_], rl_sem.at[index], left_z, go_left)
            if j == 3:
                dp_ = dpi(x, bset, c)
                tn_ = z * NB + b_
                here = jnp.logical_and(dp_ == dp, tn_ == tn)
                remote(
                    sbuf.at[k, b_],
                    frecv.at[pair],
                    f_sem.at[pair],
                    dev(dp_, tn_),
                    jnp.logical_and(is_end, jnp.logical_not(here)),
                )
                local(
                    sbuf.at[k, b_],
                    frecv.at[pair],
                    f_sem.at[pair],
                    jnp.logical_and(is_end, here),
                )

    arrived(res, res_sem)
    for p in (0, 1):
        arrived(frecv.at[p], f_sem.at[p])
    out_ref[...] = (
        res[:NROWS].astype(F32) + (frecv[0].astype(F32) + frecv[1].astype(F32))
    ).astype(BF)

    for cond, copy in pending:
        if cond is None:
            copy.wait_send()
        else:
            pl.when(cond)(copy.wait_send)


def body(
    token_ids, lengths, embed_table, norm_gain, w_query, key_value_weight, w_out, key_value_cache
):
    dp = lax.axis_index("dp")
    quarter = lax.axis_index("tensor") % NB
    tokens = jnp.pad(token_ids.T.reshape(-1), (0, 1024 - NROWS)).reshape(8, 128)
    table = embed_table.reshape(16, -1)
    gain = lax.dynamic_slice(norm_gain, (dp * 16,), (16,)).astype(F32)
    gain = jnp.broadcast_to(gain[:, None], (16, 128))
    keyval = key_value_weight.T.reshape(64, 2, 256).transpose(1, 0, 2).reshape(128, 256)
    shard = jnp.concatenate([w_query, keyval], axis=0)
    cache = key_value_cache.reshape(40, 16, 256)
    here = jnp.repeat(lax.dynamic_slice(lengths, (quarter * 10,), (10,)), 4)
    position = here + jnp.tile(jnp.arange(4, dtype=jnp.int32), 10)
    frequency = THETA ** (-(jnp.arange(64, dtype=F32) / 64))
    turn = position.astype(F32)[:, None] * frequency
    cosine = jnp.cos(turn)
    sine = jnp.sin(turn)
    cosine = jnp.concatenate([cosine, cosine], axis=1)
    sine = jnp.concatenate([-sine, sine], axis=1)
    lens = jnp.broadcast_to(here[:, None], (QROWS, 128))

    vmem = pl.BlockSpec(memory_space=pltpu.VMEM)
    anywhere = pl.BlockSpec(memory_space=pl.ANY)
    dma = pltpu.SemaphoreType.DMA
    all_tokens = pl.pallas_call(
        exchange_tokens,
        out_shape=jax.ShapeDtypeStruct((16, 8, 128), jnp.int32),
        in_specs=[vmem],
        out_specs=vmem,
        scratch_shapes=[dma((16,)), dma],
        compiler_params=pltpu.CompilerParams(collective_id=1, has_side_effects=True),
        name="exchange_tokens",
    )(tokens)
    found = pl.pallas_call(
        look_up,
        out_shape=jax.ShapeDtypeStruct((8, 2, 16, 256), BF),
        in_specs=[pl.BlockSpec(memory_space=pltpu.SMEM), vmem, vmem],
        out_specs=vmem,
        compiler_params=pltpu.CompilerParams(vmem_limit_bytes=16 * 1024 * 1024),
        name="look_up",
    )(all_tokens, table, gain)
    out = pl.pallas_call(
        kernel,
        out_shape=jax.ShapeDtypeStruct((NROWS, 256), BF),
        in_specs=[anywhere, anywhere, anywhere, anywhere, vmem, vmem, vmem],
        out_specs=vmem,
        scratch_shapes=[
            pltpu.VMEM((16, 2, 16, 256), BF),
            pltpu.VMEM((2, XROWS, 256), BF),
            pltpu.VMEM((4, NB, XROWS, 256), BF),
            pltpu.VMEM((XROWS, 256), BF),
            pltpu.VMEM((2, NX, 2, 640, 256), BF),
            pltpu.VMEM((2, NX, 2, 256, 512), BF),
            pltpu.VMEM((NB, 10, 16, 256), BF),
            pltpu.VMEM((NB, QPAD, 640), BF),
            pltpu.VMEM((2, 2, QPAD, 640), BF),
            pltpu.VMEM((2, QPAD, 512), BF),
            pltpu.VMEM((NB, QPAD, 512), BF),
            pltpu.VMEM((NROWS, 512), BF),
            pltpu.VMEM((NROWS, 512), F32),
            pltpu.VMEM((NROWS, 128), F32),
            pltpu.VMEM((NROWS, 128), F32),
            pltpu.VMEM((NROWS, 256), F32),
            pltpu.VMEM((4, NB, NROWS, 256), BF),
            pltpu.VMEM((4, NB, NROWS, 256), BF),
            pltpu.VMEM((4, NB, NROWS, 256), BF),
            pltpu.VMEM((2, NROWS, 256), BF),
            dma((192,)),
            dma,
            dma((16,)),
            dma,
            dma((32,)),
            dma((32,)),
            dma,
            dma((4,)),
            dma((4,)),
            dma((16,)),
            dma((16,)),
            dma((2,)),
        ],
        compiler_params=pltpu.CompilerParams(
            collective_id=0, has_side_effects=True, vmem_limit_bytes=56 * 1024 * 1024
        ),
        name="decode_block",
    )(found, shard, w_out, cache, cosine, sine, lens)
    return out.reshape(40, 4, 256).transpose(1, 0, 2)


def solution(mesh):
    in_specs = (
        P(None, "dp"),
        P("dp"),
        P(None, "tensor", "dp", None),
        P("tensor"),
        P("dp", "tensor"),
        P("dp", "tensor"),
        P("tensor", "dp"),
        P("dp", "tensor", None, None),
    )
    out_specs = P(None, "dp", "tensor")
    return jax.shard_map(body, mesh=mesh, in_specs=in_specs, out_specs=out_specs, check_vma=False)
```

```python
import functools
import math

import jax
import jax.numpy as jnp
import numpy as np
from jax import lax
from jax.experimental import pallas as pl
from jax.experimental.pallas import tpu as pltpu
from jax.sharding import PartitionSpec as P

EPS = 1e-06
THETA = 1000000.0
BF = jnp.bfloat16
F32 = jnp.float32

NX = 4
NZ = 8
NB = 4
QROWS = 40
QPAD = 48
NROWS = 160
XROWS = 176
HEAD = 128
FULL = 8192

MESH = pl.DeviceIdType.MESH


def kernel(
    tok_ref,
    table_ref,
    gain_ref,
    freq_ref,
    wq_ref,
    wkv_ref,
    wo_ref,
    cache_ref,
    out_ref,
    tab,
    tokv,
    toks,
    lsend,
    cos_ref,
    sin_ref,
    lrecv,
    xt,
    xb,
    res,
    wbuf,
    wobuf,
    cbuf,
    qsend,
    qrecv,
    asend,
    arecv,
    att,
    qacc,
    kvacc,
    ssq,
    acc,
    sbuf,
    rright,
    rleft,
    frecv,
    send_sem,
    loc_sem,
    tok_sem,
    l_sem,
    x_sem,
    res_sem,
    w_sem,
    wo_sem,
    c_sem,
    q_sem,
    a_sem,
    rr_sem,
    rl_sem,
    f_sem,
):
    dp = lax.axis_index("dp")
    tn = lax.axis_index("tensor")
    x = dp // 4
    yh = (dp // 2) % 2
    c = dp % 2
    z = tn // 4
    b = tn % 4
    zpar = z % 2
    match = zpar == yh
    pair = b // 2
    bset = b % 2

    def dev(dp_, tn_):
        return {"dp": dp_, "tensor": tn_}

    def dpi(x_, yh_, c_):
        return (x_ * 2 + yh_) * 2 + c_

    pending = []
    counter = [0]

    def remote(src, dst, rsem, where, cond=None):
        n = counter[0]
        counter[0] += 1
        copy = pltpu.make_async_remote_copy(
            src_ref=src,
            dst_ref=dst,
            send_sem=send_sem.at[n],
            recv_sem=rsem,
            device_id=where,
            device_id_type=MESH,
        )
        if cond is None:
            copy.start()
        else:
            pl.when(cond)(copy.start)
        pending.append((cond, copy))

    def local(src, dst, sem, cond=None):
        copy = pltpu.make_async_copy(src, dst, sem)
        if cond is None:
            copy.start()
        else:
            pl.when(cond)(copy.start)

    def arrived(dst, sem):
        pltpu.make_async_copy(dst, dst, sem).wait()

    def to(src, dst, rsem, dp_, tn_):
        here = jnp.logical_and(dp_ == dp, tn_ == tn)
        remote(src, dst, rsem, dev(dp_, tn_), jnp.logical_not(here))
        local(src, dst, rsem, here)

    xr = (x + 1) % NX
    xl = (x + NX - 1) % NX
    xo = (x + 2) % NX
    zr = (z + 1) % NZ
    zl = (z + NZ - 1) % NZ
    right_z = dev(dp, zr * NB + b)
    left_z = dev(dp, zl * NB + b)

    table_copy = pltpu.make_async_copy(table_ref, tab, loc_sem.at[0])
    table_copy.start()
    own_shard = wbuf.at[bset, x, c]
    own_sem = w_sem.at[((bset * NX + x) * 2 + c) * 2]
    local(wq_ref, own_shard.at[pl.ds(0, 512)], own_sem)
    for h in (0, 1):
        local(
            wkv_ref.at[:, pl.ds(h * 256, 256)], own_shard.at[pl.ds(512 + h * 64, 64)], own_sem
        )

    barrier = pltpu.get_barrier_semaphore()
    partners = 0
    for i in range(1, 16):
        pl.semaphore_signal(barrier, inc=1, device_id=dev((dp + i) % 16, tn), device_id_type=MESH)
        partners += 1
    for i in range(1, 8):
        if i == 4:
            continue
        u = (yh * 4 + b + i) % 8
        pl.semaphore_signal(
            barrier, inc=1, device_id=dev(dpi(x, u // 4, c), z * NB + u % 4), device_id_type=MESH
        )
        partners += 1
    for where in (right_z, left_z):
        pl.semaphore_signal(barrier, inc=1, device_id=where, device_id_type=MESH)
        partners += 1

    row40 = lax.broadcasted_iota(jnp.int32, (QROWS, 128), 0)
    lane40 = lax.broadcasted_iota(jnp.int32, (QROWS, 128), 1)
    lengths = tok_ref[4:5].astype(F32)
    length = jnp.sum(
        jnp.where(lane40 == b * 10 + row40 // 4, lengths, 0.0), axis=1, keepdims=True
    )
    turn = (length + (row40 % 4).astype(F32)) * freq_ref[...]
    cos_ref[...] = jnp.cos(turn)
    sin_ref[...] = jnp.where(lane40 < HEAD // 2, -1.0, 1.0) * jnp.sin(turn)

    pl.semaphore_wait(barrier, partners)

    for i in range(1, 16):
        remote(tok_ref, tokv.at[dp], tok_sem, dev((dp + i) % 16, tn))
    local(tok_ref, tokv.at[dp], tok_sem)

    class Gather:
        def __init__(self, buf, sem, half):
            self.buf, self.sem, self.half = buf, sem, half

        def slot(self, q, x_, c_, h=None):
            ref = self.buf.at[q, x_, c_]
            if h is None:
                return ref
            return ref.at[pl.ds(h * self.half, self.half)]

        def s(self, q, x_, c_, h=0):
            return self.sem.at[((q * NX + x_) * 2 + c_) * 2 + h]

        def send(self, src, q, x_, where):
            remote(src, self.slot(q, x_, c), self.s(q, x_, c), where)

        def first(self):
            own = (bset, x)
            src = self.slot(*own, c)
            arrived(src, self.s(*own, c))
            self.send(src, *own, dev(dp, z * NB + pair * 2 + 1 - bset))
            self.send(src, *own, dev(dpi(xr, yh, c), tn))
            self.send(src, *own, dev(dpi(xl, yh, c), tn))
            self.send(src, *own, dev(dpi(x, yh, 1 - c), tn))

        def second(self):
            q = 1 - bset
            arrived(self.slot(q, x, c), self.s(q, x, c))
            src = self.slot(q, x, c)
            self.send(src, q, x, dev(dpi(xr, yh, c), tn))
            self.send(src, q, x, dev(dpi(xl, yh, c), tn))
            self.send(src, q, x, dev(dpi(x, yh, 1 - c), tn))

        def relay(self, q):
            for x_, h, to_x in ((xl, 0, xr), (xr, 1, xl)):
                arrived(self.slot(q, x_, c), self.s(q, x_, c))
                remote(
                    self.slot(q, x_, c, h),
                    self.slot(q, x_, c, h),
                    self.s(q, x_, c, h),
                    dev(dpi(to_x, yh, c), tn),
                )
                self.send(self.slot(q, x_, c), q, x_, dev(dpi(x, yh, 1 - c), tn))

        def last(self, q):
            for h in (0, 1):
                arrived(self.slot(q, xo, c, h), self.s(q, xo, c, h))
            self.send(self.slot(q, xo, c), q, xo, dev(dpi(x, yh, 1 - c), tn))

        def finish(self):
            for q in (0, 1):
                for x_ in range(NX):
                    arrived(self.slot(q, x_, 1 - c), self.s(q, x_, 1 - c))

    wqkv = Gather(wbuf, w_sem, 320)
    wout = Gather(wobuf, wo_sem, 128)
    wqkv.first()
    local(wo_ref, wout.slot(bset, x, c), wout.s(bset, x, c))

    arrived(tokv, tok_sem)
    to_scalar = pltpu.make_async_copy(tokv, toks, loc_sem.at[1])
    to_scalar.start()
    to_scalar.wait()
    table_copy.wait()

    lane = lax.broadcasted_iota(jnp.int32, (16, 128), 1)
    wide = lax.broadcasted_iota(jnp.int32, (16, 256), 1)
    feature = lax.broadcasted_iota(jnp.int32, (16, 256), 0)
    gain_column = jnp.sum(
        jnp.where(wide == dp * 16 + feature, gain_ref[...].astype(F32), 0.0),
        axis=1,
        keepdims=True,
    )
    gain_tail = jnp.where(lane == NROWS - 128, gain_column, 0.0)
    place = x * 2 + c
    lookup_base = counter[0]
    counter[0] += 8

    def lookup_copy(e):
        dp2 = dpi(e // 2, zpar, e % 2)
        return dp2, pltpu.make_async_remote_copy(
            src_ref=lsend.at[e],
            dst_ref=lrecv.at[dp],
            send_sem=send_sem.at[lookup_base + e],
            recv_sem=l_sem,
            device_id=dev(dp2, tn),
            device_id_type=MESH,
        )

    def lookup(i, carry):
        e = (place + 1 + i) % 8

        def one_set(s, carry):
            d2 = dpi(e // 2, s, e % 2)
            for half, count in ((0, 128), (1, NROWS - 128)):
                found = jnp.zeros((16, 128), F32) if half == 0 else gain_tail
                for n in range(count):
                    row = half * 128 + n
                    token = toks[d2, row % 4, row // 4]
                    block = lax.shift_right_logical(token, 7)
                    tile = tab[:, pl.ds(block * 128, 128)].astype(F32)
                    picked = jnp.where(lane == jnp.bitwise_and(token, 127), tile, 0.0)
                    found = jnp.where(lane == n, jnp.sum(picked, axis=1, keepdims=True), found)
                lsend[e, s, :, pl.ds(half * 128, 128)] = found.astype(BF)
            return carry

        lax.fori_loop(0, 2, one_set, 0)
        dp2, copy = lookup_copy(e)
        pl.when(dp2 != dp)(copy.start)
        pl.when(dp2 == dp)(pltpu.make_async_copy(lsend.at[e], lrecv.at[dp], l_sem).start)
        return carry

    lax.fori_loop(0, 4, lookup, 0)
    wqkv.second()
    wqkv.relay(bset)
    lax.fori_loop(4, 8, lookup, 0)
    wqkv.relay(1 - bset)

    for i in range(NB):
        b2 = (b + i) % NB
        to(cache_ref.at[pl.ds(b2 * 10, 10)], cbuf.at[b], c_sem, dp, z * NB + b2)

    k_here = z // 2

    @pl.when(match)
    def _():
        arrived(lrecv, l_sem)
        for s in (0, 1):
            features = lrecv[:, s].reshape(256, 256).astype(F32)
            xt[s] = features.T[:XROWS].astype(BF)

    for s in (0, 1):
        for h in (0, 1):
            b2 = s + 2 * h
            same = b2 == b
            remote(
                xt.at[s],
                xb.at[k_here, b],
                x_sem.at[k_here * NB + b],
                dev(dp, z * NB + b2),
                jnp.logical_and(match, jnp.logical_not(same)),
            )
            local(
                xt.at[s], xb.at[k_here, b], x_sem.at[k_here * NB + b], jnp.logical_and(match, same)
            )

    def gather_z(j):
        delta = jnp.where(match, (0, 2, 6, 4)[j], (1, 7, 3, 5)[j])
        k = ((z - delta + NZ) % NZ) // 2
        for b_ in range(NB):
            reach = 4 if b_ < 2 else 3
            block = xb.at[k, b_]
            sem = x_sem.at[k * NB + b_]
            arrived(block, sem)
            if j < 3:
                remote(block, block, sem, right_z, delta < reach)
                remote(
                    block,
                    block,
                    sem,
                    left_z,
                    jnp.logical_or(
                        delta == 0, jnp.logical_and(delta > reach, 8 - delta < 7 - reach)
                    ),
                )
            else:
                remote(block, block, sem, right_z, delta < reach)
                remote(
                    block,
                    block,
                    sem,
                    left_z,
                    jnp.logical_and(delta > reach, 8 - delta < 7 - reach),
                )
        return k

    def project(k, start):
        for b_ in range(NB):
            raw = xb[k, b_].astype(F32)
            rows = raw[:NROWS]
            gain = raw[NROWS : NROWS + 1]
            scaled = (rows * gain).astype(BF)
            square = rows * rows
            square = square[:, :128] + square[:, 128:]
            c_ = b_ // 2
            h = b_ % 2
            parts = [
                jnp.dot(
                    scaled, wbuf[q, k, c_, h * 256 : h * 256 + 256], preferred_element_type=F32
                )
                for q in (0, 1)
            ]
            keyval = jnp.concatenate(
                [wbuf[q, k, c_, 512 + h * 64 : 576 + h * 64] for q in (0, 1)], axis=0
            )
            kv = lax.dot_general(
                scaled, keyval, (((1,), (1,)), ((), ())), preferred_element_type=F32
            )
            if start and b_ == 0:
                ssq[...] = square
                qacc[:, :256] = parts[0]
                qacc[:, 256:] = parts[1]
                kvacc[...] = kv
            else:
                ssq[...] += square
                qacc[:, :256] += parts[0]
                qacc[:, 256:] += parts[1]
                kvacc[...] += kv

    wqkv.last(bset)
    wqkv.last(1 - bset)
    wout.first()
    ks = [gather_z(0)]
    ks.append(gather_z(1))
    wqkv.finish()
    wout.second()
    project(ks[0], True)
    ks.append(gather_z(2))
    project(ks[1], False)
    wout.relay(bset)
    ks.append(gather_z(3))
    project(ks[2], False)
    project(ks[3], False)

    for_partner = 1 - zpar
    remote(xt.at[for_partner], res, res_sem, dev(dpi(x, for_partner, c), tn), match)
    local(xt.at[yh], res, res_sem, match)

    diagonal = row40 == lane40
    row8 = lax.broadcasted_iota(jnp.int32, (8, 128), 0)
    for i in range(NB):
        total = jnp.sum(ssq[i * QROWS : (i + 1) * QROWS], axis=1, keepdims=True)
        flat = jnp.sum(jnp.where(diagonal, total, 0.0), axis=0, keepdims=True)
        high = flat.astype(BF).astype(F32)
        low = flat - high
        tail = jnp.where(row8 == 0, high, jnp.where(row8 == 1, low, 0.0))
        tail = jnp.concatenate([tail, jnp.zeros((8, 512), F32)], axis=1)
        body_rows = jnp.concatenate(
            [qacc[i * QROWS : (i + 1) * QROWS], kvacc[i * QROWS : (i + 1) * QROWS]], axis=1
        )
        qsend[i] = jnp.concatenate([body_rows, tail], axis=0).astype(BF)
        to(
            qsend.at[i],
            qrecv.at[yh, pair],
            q_sem.at[yh * 2 + pair],
            dpi(x, bset, c),
            z * NB + i,
        )

    wout.relay(1 - bset)

    for i in range(NB):
        arrived(qrecv.at[i // 2, i % 2], q_sem.at[i])
    arrived(cbuf, c_sem)

    tails = qrecv[0, 0, 32:QPAD, :128].astype(F32) + qrecv[1, 0, 32:QPAD, :128].astype(F32)
    flat = tails[8:9] + tails[9:10]
    total = jnp.sum(jnp.where(diagonal, flat, 0.0), axis=1, keepdims=True)
    factor = lax.rsqrt(total * (1.0 / FULL) + EPS)
    cosine = cos_ref[...]
    sine = sin_ref[...]

    def rope(u):
        return u * cosine + pltpu.roll(u, HEAD // 2, 1) * sine

    heads = []
    news = []
    for p in (0, 1):
        both = qrecv[0, p].astype(F32) + qrecv[1, p].astype(F32)
        both = both[:QROWS] * factor
        for i in range(4):
            heads.append(rope(both[:, i * HEAD : (i + 1) * HEAD]))
        news.append(both[:, 512:640])
    query = jnp.concatenate(heads, axis=0).astype(BF)
    no_rows = jnp.zeros((128 - QROWS, HEAD), F32)
    key_new = rope(news[0].astype(BF).astype(F32))
    key_new = jnp.concatenate([key_new, no_rows], axis=0).astype(BF)
    value_new = jnp.concatenate([news[1], no_rows], axis=0).astype(BF)
    keys = cbuf[:, :, :, :HEAD].reshape(640, HEAD)
    values = cbuf[:, :, :, HEAD:].reshape(640, HEAD)

    contract_last = (((1,), (1,)), ((), ()))
    inv_root = 1.0 / math.sqrt(HEAD)
    scores_old = lax.dot_general(query, keys, contract_last, preferred_element_type=F32) * inv_root
    scores_new = (
        lax.dot_general(query, key_new, contract_last, preferred_element_type=F32) * inv_root
    )
    col = lax.broadcasted_iota(jnp.int32, (QROWS, 640), 1)
    row = lax.broadcasted_iota(jnp.int32, (QROWS, 640), 0) // 4
    within = col % 160
    position = (col // 160) * 16 + within % 16
    old_ok = jnp.logical_and(within // 16 == row, position.astype(F32) < length)
    new_ok = jnp.logical_and(
        lane40 // 4 == row40 // 4, jnp.logical_and(lane40 <= row40, lane40 < QROWS)
    )
    old_bias = jnp.where(old_ok, 0.0, -1e30)
    new_bias = jnp.where(new_ok, 0.0, -1e30)
    old_bias = jnp.concatenate([old_bias] * 8, axis=0)
    new_bias = jnp.concatenate([new_bias] * 8, axis=0)
    scores_old = jnp.where(old_bias == 0.0, scores_old, -1e30)
    scores_new = jnp.where(new_bias == 0.0, scores_new, -1e30)
    top = jnp.maximum(
        jnp.max(scores_old, axis=1, keepdims=True), jnp.max(scores_new, axis=1, keepdims=True)
    )
    exp_old = jnp.exp(scores_old - top)
    exp_new = jnp.exp(scores_new - top)
    totals = jnp.sum(exp_old, axis=1, keepdims=True) + jnp.sum(exp_new, axis=1, keepdims=True)
    probs_old = (exp_old / totals).astype(BF)
    probs_new = (exp_new / totals).astype(BF)
    attended = jnp.dot(probs_old, values, preferred_element_type=F32)
    attended = attended + jnp.dot(probs_new, value_new, preferred_element_type=F32)
    for p in (0, 1):
        side = jnp.concatenate(
            [attended[(4 * p + i) * QROWS : (4 * p + i + 1) * QROWS] for i in range(4)], axis=1
        )
        asend[p] = jnp.concatenate([side, jnp.zeros((QPAD - QROWS, 512), F32)], axis=0).astype(BF)
        for y_ in (0, 1):
            to(asend.at[p], arecv.at[b], a_sem.at[b], dpi(x, y_, c), z * NB + p * 2 + yh)

    wout.last(bset)
    wout.last(1 - bset)
    wout.finish()
    for i in range(NB):
        arrived(arecv.at[i], a_sem.at[i])
    att[...] = jnp.concatenate(
        [arecv[i].astype(F32)[:QROWS] for i in range(NB)], axis=0
    ).astype(BF)

    for j in range(4):
        delta = jnp.where(match, (4, 2, 6, 0)[j], (3, 5, 1, 7)[j])
        k = ((z + delta) % NZ) // 2
        is_end = delta == 0
        for b_ in range(NB):
            reach = 4 if b_ < 2 else 3
            c_ = b_ // 2
            h = b_ % 2
            part = jnp.dot(
                att[:, :256],
                wobuf[0, k, c_, :, h * 256 : h * 256 + 256],
                preferred_element_type=F32,
            )
            part = part + jnp.dot(
                att[:, 256:],
                wobuf[1, k, c_, :, h * 256 : h * 256 + 256],
                preferred_element_type=F32,
            )
            acc[...] = part
            go_right = jnp.logical_and(delta >= 1, delta <= reach)
            go_left = delta > reach
            from_left = delta + 1 <= reach
            from_right = jnp.logical_or(delta > reach + 1, is_end)
            index = k * NB + b_

            @pl.when(from_left)
            def _(index=index, k=k, b_=b_):
                arrived(rright.at[k, b_], rr_sem.at[index])
                acc[...] += rright[k, b_].astype(F32)

            @pl.when(from_right)
            def _(index=index, k=k, b_=b_):
                arrived(rleft.at[k, b_], rl_sem.at[index])
                acc[...] += rleft[k, b_].astype(F32)

            sbuf[k, b_] = acc[...].astype(BF)
            remote(sbuf.at[k, b_], rright.at[k, b_], rr_sem.at[index], right_z, go_right)
            remote(sbuf.at[k, b_], rleft.at[k, b_], rl_sem.at[index], left_z, go_left)
            if j == 3:
                dp_ = dpi(x, bset, c)
                tn_ = z * NB + b_
                here = jnp.logical_and(dp_ == dp, tn_ == tn)
                remote(
                    sbuf.at[k, b_],
                    frecv.at[pair],
                    f_sem.at[pair],
                    dev(dp_, tn_),
                    jnp.logical_and(is_end, jnp.logical_not(here)),
                )
                local(
                    sbuf.at[k, b_],
                    frecv.at[pair],
                    f_sem.at[pair],
                    jnp.logical_and(is_end, here),
                )

    arrived(res, res_sem)
    for p in (0, 1):
        arrived(frecv.at[p], f_sem.at[p])
    hidden = res[:NROWS].astype(F32) + (frecv[0].astype(F32) + frecv[1].astype(F32))
    hidden = jnp.concatenate([hidden, jnp.zeros((256 - NROWS, 256), F32)], axis=0).astype(BF)
    to_row = lax.broadcasted_iota(jnp.int32, (NROWS, 256), 0)
    from_row = lax.broadcasted_iota(jnp.int32, (NROWS, 256), 1)
    order = jnp.where(from_row == (to_row % 40) * 4 + to_row // 40, 1.0, 0.0).astype(BF)
    out_ref[...] = jnp.dot(order, hidden, preferred_element_type=F32).astype(BF)

    for cond, copy in pending:
        if cond is None:
            copy.wait_send()
        else:
            pl.when(cond)(copy.wait_send)

    def lookup_sent(e, carry):
        dp2, copy = lookup_copy(e)
        pl.when(dp2 != dp)(copy.wait_send)
        return carry

    lax.fori_loop(0, 8, lookup_sent, 0)


def body(
    token_ids, lengths, embed_table, norm_gain, w_query, key_value_weight, w_out, key_value_cache
):
    numbers = jnp.concatenate([token_ids, lengths[None]], axis=0)
    numbers = jnp.pad(numbers, ((0, 3), (0, 88)))
    table = embed_table.reshape(16, -1)
    gain = norm_gain.reshape(1, -1)
    frequency = THETA ** (-(np.arange(64) / 64))
    frequency = jnp.asarray(np.concatenate([frequency, frequency])[None], F32)
    keyval = key_value_weight.T
    cache = key_value_cache.reshape(40, 16, 256)

    vmem = pl.BlockSpec(memory_space=pltpu.VMEM)
    anywhere = pl.BlockSpec(memory_space=pl.ANY)
    dma = pltpu.SemaphoreType.DMA
    out = pl.pallas_call(
        kernel,
        out_shape=jax.ShapeDtypeStruct((NROWS, 256), BF),
        in_specs=[vmem, anywhere, vmem, vmem, anywhere, anywhere, anywhere, anywhere],
        out_specs=vmem,
        scratch_shapes=[
            pltpu.VMEM((16, 81920), BF),
            pltpu.VMEM((16, 8, 128), jnp.int32),
            pltpu.SMEM((16, 8, 128), jnp.int32),
            pltpu.VMEM((8, 2, 16, 256), BF),
            pltpu.VMEM((QROWS, HEAD), F32),
            pltpu.VMEM((QROWS, HEAD), F32),
            pltpu.VMEM((16, 2, 16, 256), BF),
            pltpu.VMEM((2, XROWS, 256), BF),
            pltpu.VMEM((4, NB, XROWS, 256), BF),
            pltpu.VMEM((XROWS, 256), BF),
            pltpu.VMEM((2, NX, 2, 640, 256), BF),
            pltpu.VMEM((2, NX, 2, 256, 512), BF),
            pltpu.VMEM((NB, 10, 16, 256), BF),
            pltpu.VMEM((NB, QPAD, 640), BF),
            pltpu.VMEM((2, 2, QPAD, 640), BF),
            pltpu.VMEM((2, QPAD, 512), BF),
            pltpu.VMEM((NB, QPAD, 512), BF),
            pltpu.VMEM((NROWS, 512), BF),
            pltpu.VMEM((NROWS, 512), F32),
            pltpu.VMEM((NROWS, 128), F32),
            pltpu.VMEM((NROWS, 128), F32),
            pltpu.VMEM((NROWS, 256), F32),
            pltpu.VMEM((4, NB, NROWS, 256), BF),
            pltpu.VMEM((4, NB, NROWS, 256), BF),
            pltpu.VMEM((4, NB, NROWS, 256), BF),
            pltpu.VMEM((2, NROWS, 256), BF),
            dma((192,)),
            dma((2,)),
            dma,
            dma,
            dma((16,)),
            dma,
            dma((32,)),
            dma((32,)),
            dma,
            dma((4,)),
            dma((4,)),
            dma((16,)),
            dma((16,)),
            dma((2,)),
        ],
        compiler_params=pltpu.CompilerParams(
            collective_id=0, has_side_effects=True, vmem_limit_bytes=56 * 1024 * 1024
        ),
        name="decode_block",
    )(numbers, table, gain, frequency, w_query, keyval, w_out, cache)
    return out.reshape(4, 40, 256)


def solution(mesh):
    in_specs = (
        P(None, "dp"),
        P("dp"),
        P(None, "tensor", "dp", None),
        P("tensor"),
        P("dp", "tensor"),
        P("dp", "tensor"),
        P("tensor", "dp"),
        P("dp", "tensor", None, None),
    )
    out_specs = P(None, "dp", "tensor")
    return jax.shard_map(body, mesh=mesh, in_specs=in_specs, out_specs=out_specs, check_vma=False)
```

```python
import functools
import math

import jax
import jax.numpy as jnp
import numpy as np
from jax import lax
from jax.experimental import pallas as pl
from jax.experimental.pallas import tpu as pltpu
from jax.sharding import PartitionSpec as P

EPS = 1e-06
THETA = 1000000.0
BF = jnp.bfloat16
F32 = jnp.float32

NX = 4
NZ = 8
NB = 4
QROWS = 40
QPAD = 48
NROWS = 160
XROWS = 176
HEAD = 128
FULL = 8192

MESH = pl.DeviceIdType.MESH


def kernel(
    tok_ref,
    len_ref,
    table_ref,
    gain_ref,
    freq_ref,
    wq_ref,
    wkv_ref,
    wo_ref,
    cache_ref,
    out_ref,
    tab,
    tokv,
    toks,
    lsend,
    cos_ref,
    sin_ref,
    lrecv,
    xt,
    xb,
    res,
    wbuf,
    wobuf,
    cbuf,
    qsend,
    qrecv,
    asend,
    arecv,
    att,
    qacc,
    kvacc,
    ssq,
    acc,
    sbuf,
    rright,
    rleft,
    frecv,
    send_sem,
    loc_sem,
    tok_sem,
    l_sem,
    x_sem,
    res_sem,
    w_sem,
    wo_sem,
    c_sem,
    q_sem,
    a_sem,
    rr_sem,
    rl_sem,
    f_sem,
):
    dp = lax.axis_index("dp")
    tn = lax.axis_index("tensor")
    x = dp // 4
    yh = (dp // 2) % 2
    c = dp % 2
    z = tn // 4
    b = tn % 4
    zpar = z % 2
    match = zpar == yh
    pair = b // 2
    bset = b % 2

    def dev(dp_, tn_):
        return {"dp": dp_, "tensor": tn_}

    def dpi(x_, yh_, c_):
        return (x_ * 2 + yh_) * 2 + c_

    pending = []
    counter = [0]

    def remote(src, dst, rsem, where, cond=None):
        n = counter[0]
        counter[0] += 1
        copy = pltpu.make_async_remote_copy(
            src_ref=src,
            dst_ref=dst,
            send_sem=send_sem.at[n],
            recv_sem=rsem,
            device_id=where,
            device_id_type=MESH,
        )
        if cond is None:
            copy.start()
        else:
            pl.when(cond)(copy.start)
        pending.append((cond, copy))

    def local(src, dst, sem, cond=None):
        copy = pltpu.make_async_copy(src, dst, sem)
        if cond is None:
            copy.start()
        else:
            pl.when(cond)(copy.start)

    def arrived(dst, sem):
        pltpu.make_async_copy(dst, dst, sem).wait()

    def to(src, dst, rsem, dp_, tn_):
        here = jnp.logical_and(dp_ == dp, tn_ == tn)
        remote(src, dst, rsem, dev(dp_, tn_), jnp.logical_not(here))
        local(src, dst, rsem, here)

    xr = (x + 1) % NX
    xl = (x + NX - 1) % NX
    xo = (x + 2) % NX
    zr = (z + 1) % NZ
    zl = (z + NZ - 1) % NZ
    right_z = dev(dp, zr * NB + b)
    left_z = dev(dp, zl * NB + b)

    table_copy = pltpu.make_async_copy(table_ref, tab, loc_sem.at[0])
    table_copy.start()
    own_shard = wbuf.at[bset, x, c]
    own_sem = w_sem.at[((bset * NX + x) * 2 + c) * 2]
    local(wq_ref, own_shard.at[pl.ds(0, 512)], own_sem)
    for h in (0, 1):
        local(
            wkv_ref.at[:, pl.ds(h * 256, 256)], own_shard.at[pl.ds(512 + h * 64, 64)], own_sem
        )

    barrier = pltpu.get_barrier_semaphore()
    partners = 0
    for i in range(1, 16):
        pl.semaphore_signal(barrier, inc=1, device_id=dev((dp + i) % 16, tn), device_id_type=MESH)
        partners += 1
    for i in range(1, 8):
        if i == 4:
            continue
        u = (yh * 4 + b + i) % 8
        pl.semaphore_signal(
            barrier, inc=1, device_id=dev(dpi(x, u // 4, c), z * NB + u % 4), device_id_type=MESH
        )
        partners += 1
    for where in (right_z, left_z):
        pl.semaphore_signal(barrier, inc=1, device_id=where, device_id_type=MESH)
        partners += 1

    row40 = lax.broadcasted_iota(jnp.int32, (QROWS, 128), 0)
    lane40 = lax.broadcasted_iota(jnp.int32, (QROWS, 128), 1)
    lengths = len_ref[...].astype(F32)
    row_of = lax.broadcasted_iota(jnp.int32, (QROWS, 40), 0) // 4 + b * 10
    all_rows = lax.broadcasted_iota(jnp.int32, (QROWS, 40), 1)
    length = jnp.sum(jnp.where(all_rows == row_of, lengths, 0.0), axis=1, keepdims=True)
    turn = (length + (row40 % 4).astype(F32)) * freq_ref[...]
    cos_ref[...] = jnp.cos(turn)
    sin_ref[...] = jnp.where(lane40 < HEAD // 2, -1.0, 1.0) * jnp.sin(turn)

    pl.semaphore_wait(barrier, partners)

    for i in range(1, 16):
        remote(tok_ref, tokv.at[dp], tok_sem, dev((dp + i) % 16, tn))
    local(tok_ref, tokv.at[dp], tok_sem)

    class Gather:
        def __init__(self, buf, sem, half):
            self.buf, self.sem, self.half = buf, sem, half

        def slot(self, q, x_, c_, h=None):
            ref = self.buf.at[q, x_, c_]
            if h is None:
                return ref
            return ref.at[pl.ds(h * self.half, self.half)]

        def s(self, q, x_, c_, h=0):
            return self.sem.at[((q * NX + x_) * 2 + c_) * 2 + h]

        def send(self, src, q, x_, where):
            remote(src, self.slot(q, x_, c), self.s(q, x_, c), where)

        def first(self):
            own = (bset, x)
            src = self.slot(*own, c)
            arrived(src, self.s(*own, c))
            self.send(src, *own, dev(dp, z * NB + pair * 2 + 1 - bset))
            self.send(src, *own, dev(dpi(xr, yh, c), tn))
            self.send(src, *own, dev(dpi(xl, yh, c), tn))
            self.send(src, *own, dev(dpi(x, yh, 1 - c), tn))

        def second(self):
            q = 1 - bset
            arrived(self.slot(q, x, c), self.s(q, x, c))
            src = self.slot(q, x, c)
            self.send(src, q, x, dev(dpi(xr, yh, c), tn))
            self.send(src, q, x, dev(dpi(xl, yh, c), tn))
            self.send(src, q, x, dev(dpi(x, yh, 1 - c), tn))

        def relay(self, q):
            for x_, h, to_x in ((xl, 0, xr), (xr, 1, xl)):
                arrived(self.slot(q, x_, c), self.s(q, x_, c))
                remote(
                    self.slot(q, x_, c, h),
                    self.slot(q, x_, c, h),
                    self.s(q, x_, c, h),
                    dev(dpi(to_x, yh, c), tn),
                )
                self.send(self.slot(q, x_, c), q, x_, dev(dpi(x, yh, 1 - c), tn))

        def last(self, q):
            for h in (0, 1):
                arrived(self.slot(q, xo, c, h), self.s(q, xo, c, h))
            self.send(self.slot(q, xo, c), q, xo, dev(dpi(x, yh, 1 - c), tn))

        def finish(self):
            for q in (0, 1):
                for x_ in range(NX):
                    arrived(self.slot(q, x_, 1 - c), self.s(q, x_, 1 - c))

    wqkv = Gather(wbuf, w_sem, 320)
    wout = Gather(wobuf, wo_sem, 128)
    wqkv.first()
    local(wo_ref, wout.slot(bset, x, c), wout.s(bset, x, c))

    arrived(tokv, tok_sem)
    to_scalar = pltpu.make_async_copy(tokv, toks, loc_sem.at[1])
    to_scalar.start()
    to_scalar.wait()
    table_copy.wait()

    lane = lax.broadcasted_iota(jnp.int32, (16, 128), 1)
    wide = lax.broadcasted_iota(jnp.int32, (16, 256), 1)
    feature = lax.broadcasted_iota(jnp.int32, (16, 256), 0)
    gain_column = jnp.sum(
        jnp.where(wide == dp * 16 + feature, gain_ref[...].astype(F32), 0.0),
        axis=1,
        keepdims=True,
    )
    gain_tail = jnp.where(lane == NROWS - 128, gain_column, 0.0)
    place = x * 2 + c
    lookup_base = counter[0]
    counter[0] += 8

    def lookup_copy(e):
        dp2 = dpi(e // 2, zpar, e % 2)
        return dp2, pltpu.make_async_remote_copy(
            src_ref=lsend.at[e],
            dst_ref=lrecv.at[dp],
            send_sem=send_sem.at[lookup_base + e],
            recv_sem=l_sem,
            device_id=dev(dp2, tn),
            device_id_type=MESH,
        )

    def lookup(i, carry):
        e = (place + 1 + i) % 8

        def one_set(s, carry):
            d2 = dpi(e // 2, s, e % 2)
            for half, count in ((0, 128), (1, NROWS - 128)):
                found = jnp.zeros((16, 128), F32) if half == 0 else gain_tail
                for n in range(count):
                    row = half * 128 + n
                    token = toks[d2, row % 4, row // 4]
                    block = lax.shift_right_logical(token, 7)
                    tile = tab[:, pl.ds(block * 128, 128)].astype(F32)
                    picked = jnp.where(lane == jnp.bitwise_and(token, 127), tile, 0.0)
                    found = jnp.where(lane == n, jnp.sum(picked, axis=1, keepdims=True), found)
                lsend[e, s, :, pl.ds(half * 128, 128)] = found.astype(BF)
            return carry

        lax.fori_loop(0, 2, one_set, 0)
        dp2, copy = lookup_copy(e)
        pl.when(dp2 != dp)(copy.start)
        pl.when(dp2 == dp)(pltpu.make_async_copy(lsend.at[e], lrecv.at[dp], l_sem).start)
        return carry

    lax.fori_loop(0, 4, lookup, 0)
    wqkv.second()
    wqkv.relay(bset)
    lax.fori_loop(4, 8, lookup, 0)
    wqkv.relay(1 - bset)

    k_here = z // 2

    pl.when(match)(lambda: arrived(lrecv, l_sem))
    for s in (0, 1):

        @pl.when(match)
        def _(s=s):
            features = lrecv[:, s].reshape(256, 256).astype(F32)
            xt[s] = features.T[:XROWS].astype(BF)

        for h in (0, 1):
            b2 = s + 2 * h
            here = b2 == b
            dst = xb.at[k_here, b]
            sem = x_sem.at[k_here * NB + b]
            remote(
                xt.at[s],
                dst,
                sem,
                dev(dp, z * NB + b2),
                jnp.logical_and(match, jnp.logical_not(here)),
            )
            local(xt.at[s], dst, sem, jnp.logical_and(match, here))

    def by_b(values):
        return jnp.where(
            b == 0, values[0], jnp.where(b == 1, values[1], jnp.where(b == 2, values[2], values[3]))
        )

    nearest = [by_b(v) for v in ((0, 1, 2, 3), (1, 0, 3, 2), (2, 2, 1, 1), (3, 3, 0, 0))]
    if_match = [(0, i) for i in range(4)]
    if_match += [(d, i) for i in range(4) for d in (2, 6)]
    if_match += [(4, i) for i in range(4)]
    if_not = [(d, i) for i in range(4) for d in (1, 7)]
    if_not += [(d, i) for i in range(4) for d in (3, 5)]
    blocks = []
    for (d_m, i_m), (d_n, i_n) in zip(if_match, if_not):
        delta = jnp.where(match, d_m, d_n)
        b_ = jnp.where(match, nearest[i_m], nearest[i_n])
        blocks.append((delta, ((z - delta + NZ) % NZ) // 2, b_))

    def forward(n):
        delta, k, b_ = blocks[n]
        reach = jnp.where(b_ < 2, 4, 3)
        block = xb.at[k, b_]
        sem = x_sem.at[k * NB + b_]
        arrived(block, sem)
        if n < 4:
            onward = delta == 0
        else:
            onward = False
        onward = jnp.logical_or(
            onward, jnp.logical_and(delta > reach, 8 - delta < 7 - reach)
        )
        remote(block, block, sem, right_z, delta < reach)
        remote(block, block, sem, left_z, onward)

    def project(n):
        _, k, b_ = blocks[n]
        c_ = b_ // 2
        h = b_ % 2
        raw = xb[k, b_].astype(F32)
        rows = raw[:NROWS]
        gain = raw[NROWS : NROWS + 1]
        scaled = (rows * gain).astype(BF)
        square = rows * rows
        square = square[:, :128] + square[:, 128:]
        parts = [
            jnp.dot(scaled, wbuf[q, k, c_, pl.ds(h * 256, 256)], preferred_element_type=F32)
            for q in (0, 1)
        ]
        keyval = jnp.concatenate(
            [wbuf[q, k, c_, pl.ds(512 + h * 64, 64)] for q in (0, 1)], axis=0
        )
        kv = lax.dot_general(
            scaled, keyval, (((1,), (1,)), ((), ())), preferred_element_type=F32
        )
        if n == 0:
            ssq[...] = square
            qacc[:, :256] = parts[0]
            qacc[:, 256:] = parts[1]
            kvacc[...] = kv
        else:
            ssq[...] += square
            qacc[:, :256] += parts[0]
            qacc[:, 256:] += parts[1]
            kvacc[...] += kv

    wqkv.last(bset)
    wqkv.last(1 - bset)
    for n in range(4):
        forward(n)
    wqkv.finish()
    wout.first()
    for n in range(4):
        project(n)
    for n in range(4, 16):
        forward(n)
        if n == 6:
            for i in range(NB):
                b2 = (b + i) % NB
                to(cache_ref.at[pl.ds(b2 * 10, 10)], cbuf.at[b], c_sem, dp, z * NB + b2)
        if n == 8:
            for_partner = 1 - zpar
            remote(xt.at[for_partner], res, res_sem, dev(dpi(x, for_partner, c), tn), match)
            local(xt.at[yh], res, res_sem, match)
        if n == 10:
            wout.second()
        if n == 14:
            wout.relay(bset)
        project(n)

    diagonal = row40 == lane40
    row8 = lax.broadcasted_iota(jnp.int32, (8, 128), 0)
    for i in range(NB):
        total = jnp.sum(ssq[i * QROWS : (i + 1) * QROWS], axis=1, keepdims=True)
        flat = jnp.sum(jnp.where(diagonal, total, 0.0), axis=0, keepdims=True)
        high = flat.astype(BF).astype(F32)
        low = flat - high
        tail = jnp.where(row8 == 0, high, jnp.where(row8 == 1, low, 0.0))
        tail = jnp.concatenate([tail, jnp.zeros((8, 512), F32)], axis=1)
        body_rows = jnp.concatenate(
            [qacc[i * QROWS : (i + 1) * QROWS], kvacc[i * QROWS : (i + 1) * QROWS]], axis=1
        )
        qsend[i] = jnp.concatenate([body_rows, tail], axis=0).astype(BF)
        to(
            qsend.at[i],
            qrecv.at[yh, pair],
            q_sem.at[yh * 2 + pair],
            dpi(x, bset, c),
            z * NB + i,
        )

    wout.relay(1 - bset)

    for i in range(NB):
        arrived(qrecv.at[i // 2, i % 2], q_sem.at[i])
    arrived(cbuf, c_sem)

    tails = qrecv[0, 0, 32:QPAD, :128].astype(F32) + qrecv[1, 0, 32:QPAD, :128].astype(F32)
    flat = tails[8:9] + tails[9:10]
    total = jnp.sum(jnp.where(diagonal, flat, 0.0), axis=1, keepdims=True)
    factor = lax.rsqrt(total * (1.0 / FULL) + EPS)
    cosine = cos_ref[...]
    sine = sin_ref[...]

    def rope(u):
        return u * cosine + pltpu.roll(u, HEAD // 2, 1) * sine

    heads = []
    news = []
    for p in (0, 1):
        both = qrecv[0, p].astype(F32) + qrecv[1, p].astype(F32)
        both = both[:QROWS] * factor
        for i in range(4):
            heads.append(rope(both[:, i * HEAD : (i + 1) * HEAD]))
        news.append(both[:, 512:640])
    query = jnp.concatenate(heads, axis=0).astype(BF)
    no_rows = jnp.zeros((128 - QROWS, HEAD), F32)
    key_new = rope(news[0].astype(BF).astype(F32))
    key_new = jnp.concatenate([key_new, no_rows], axis=0).astype(BF)
    value_new = jnp.concatenate([news[1], no_rows], axis=0).astype(BF)
    keys = cbuf[:, :, :, :HEAD].reshape(640, HEAD)
    values = cbuf[:, :, :, HEAD:].reshape(640, HEAD)

    contract_last = (((1,), (1,)), ((), ()))
    inv_root = 1.0 / math.sqrt(HEAD)
    scores_old = lax.dot_general(query, keys, contract_last, preferred_element_type=F32) * inv_root
    scores_new = (
        lax.dot_general(query, key_new, contract_last, preferred_element_type=F32) * inv_root
    )
    col = lax.broadcasted_iota(jnp.int32, (QROWS, 640), 1)
    row = lax.broadcasted_iota(jnp.int32, (QROWS, 640), 0) // 4
    within = col % 160
    position = (col // 160) * 16 + within % 16
    old_ok = jnp.logical_and(within // 16 == row, position.astype(F32) < length)
    new_ok = jnp.logical_and(
        lane40 // 4 == row40 // 4, jnp.logical_and(lane40 <= row40, lane40 < QROWS)
    )
    old_bias = jnp.where(old_ok, 0.0, -1e30)
    new_bias = jnp.where(new_ok, 0.0, -1e30)
    old_bias = jnp.concatenate([old_bias] * 8, axis=0)
    new_bias = jnp.concatenate([new_bias] * 8, axis=0)
    scores_old = jnp.where(old_bias == 0.0, scores_old, -1e30)
    scores_new = jnp.where(new_bias == 0.0, scores_new, -1e30)
    top = jnp.maximum(
        jnp.max(scores_old, axis=1, keepdims=True), jnp.max(scores_new, axis=1, keepdims=True)
    )
    exp_old = jnp.exp(scores_old - top)
    exp_new = jnp.exp(scores_new - top)
    totals = jnp.sum(exp_old, axis=1, keepdims=True) + jnp.sum(exp_new, axis=1, keepdims=True)
    probs_old = (exp_old / totals).astype(BF)
    probs_new = (exp_new / totals).astype(BF)
    attended = jnp.dot(probs_old, values, preferred_element_type=F32)
    attended = attended + jnp.dot(probs_new, value_new, preferred_element_type=F32)
    for p in (0, 1):
        side = jnp.concatenate(
            [attended[(4 * p + i) * QROWS : (4 * p + i + 1) * QROWS] for i in range(4)], axis=1
        )
        asend[p] = jnp.concatenate([side, jnp.zeros((QPAD - QROWS, 512), F32)], axis=0).astype(BF)
        for y_ in (0, 1):
            to(asend.at[p], arecv.at[b], a_sem.at[b], dpi(x, y_, c), z * NB + p * 2 + yh)

    wout.last(bset)
    wout.last(1 - bset)
    wout.finish()
    for i in range(NB):
        arrived(arecv.at[i], a_sem.at[i])
    att[...] = jnp.concatenate(
        [arecv[i].astype(F32)[:QROWS] for i in range(NB)], axis=0
    ).astype(BF)

    cross = ((2, 0), (3, 1), (0, 2), (1, 3))
    if_match = [(4, i) for i in range(4)]
    if_match += [item for i, j in cross for item in ((2, i), (6, j))]
    if_match += [(0, i) for i in (2, 0, 3, 1)]
    if_not = [item for i, j in cross for item in ((3, i), (5, j))]
    if_not += [item for i, j in cross for item in ((1, i), (7, j))]
    for n in range(16):
        (d_m, i_m), (d_n, i_n) = if_match[n], if_not[n]
        delta = jnp.where(match, d_m, d_n)
        b_ = jnp.where(match, i_m, i_n)
        k = ((z + delta) % NZ) // 2
        reach = jnp.where(b_ < 2, 4, 3)
        is_end = delta == 0
        c_ = b_ // 2
        h = b_ % 2
        part = jnp.dot(
            att[:, :256], wobuf[0, k, c_, :, pl.ds(h * 256, 256)], preferred_element_type=F32
        )
        acc[...] = part + jnp.dot(
            att[:, 256:], wobuf[1, k, c_, :, pl.ds(h * 256, 256)], preferred_element_type=F32
        )
        from_left = delta + 1 <= reach
        from_right = jnp.logical_or(delta > reach + 1, is_end)
        index = k * NB + b_

        @pl.when(from_left)
        def _(index=index, k=k, b_=b_):
            arrived(rright.at[k, b_], rr_sem.at[index])
            acc[...] += rright[k, b_].astype(F32)

        @pl.when(from_right)
        def _(index=index, k=k, b_=b_):
            arrived(rleft.at[k, b_], rl_sem.at[index])
            acc[...] += rleft[k, b_].astype(F32)

        src = sbuf.at[k, b_]
        src[...] = acc[...].astype(BF)
        remote(
            src,
            rright.at[k, b_],
            rr_sem.at[index],
            right_z,
            jnp.logical_and(delta >= 1, delta <= reach),
        )
        remote(src, rleft.at[k, b_], rl_sem.at[index], left_z, delta > reach)
        if n >= 12:
            dp_ = dpi(x, bset, c)
            tn_ = z * NB + b_
            here = jnp.logical_and(dp_ == dp, tn_ == tn)
            remote(
                src,
                frecv.at[pair],
                f_sem.at[pair],
                dev(dp_, tn_),
                jnp.logical_and(is_end, jnp.logical_not(here)),
            )
            local(src, frecv.at[pair], f_sem.at[pair], jnp.logical_and(is_end, here))

    arrived(res, res_sem)
    for p in (0, 1):
        arrived(frecv.at[p], f_sem.at[p])
    hidden = res[:NROWS].astype(F32) + (frecv[0].astype(F32) + frecv[1].astype(F32))
    hidden = jnp.concatenate([hidden, jnp.zeros((256 - NROWS, 256), F32)], axis=0).astype(BF)
    to_row = lax.broadcasted_iota(jnp.int32, (NROWS, 256), 0)
    from_row = lax.broadcasted_iota(jnp.int32, (NROWS, 256), 1)
    order = jnp.where(from_row == (to_row % 40) * 4 + to_row // 40, 1.0, 0.0).astype(BF)
    out_ref[...] = jnp.dot(order, hidden, preferred_element_type=F32).astype(BF)

    for cond, copy in pending:
        if cond is None:
            copy.wait_send()
        else:
            pl.when(cond)(copy.wait_send)

    def lookup_sent(e, carry):
        dp2, copy = lookup_copy(e)
        pl.when(dp2 != dp)(copy.wait_send)
        return carry

    lax.fori_loop(0, 8, lookup_sent, 0)


def body(
    token_ids, lengths, embed_table, norm_gain, w_query, key_value_weight, w_out, key_value_cache
):
    table = embed_table.reshape(16, -1)
    gain = norm_gain.reshape(1, -1)
    frequency = THETA ** (-(np.arange(64) / 64))
    frequency = jnp.asarray(np.concatenate([frequency, frequency])[None], F32)
    keyval = key_value_weight.T
    cache = key_value_cache.reshape(40, 16, 256)

    vmem = pl.BlockSpec(memory_space=pltpu.VMEM)
    anywhere = pl.BlockSpec(memory_space=pl.ANY)
    dma = pltpu.SemaphoreType.DMA
    out = pl.pallas_call(
        kernel,
        out_shape=jax.ShapeDtypeStruct((NROWS, 256), BF),
        in_specs=[vmem, vmem, anywhere, vmem, vmem, anywhere, anywhere, anywhere, anywhere],
        out_specs=vmem,
        scratch_shapes=[
            pltpu.VMEM((16, 81920), BF),
            pltpu.VMEM((16, 4, 40), jnp.int32),
            pltpu.SMEM((16, 4, 40), jnp.int32),
            pltpu.VMEM((8, 2, 16, 256), BF),
            pltpu.VMEM((QROWS, HEAD), F32),
            pltpu.VMEM((QROWS, HEAD), F32),
            pltpu.VMEM((16, 2, 16, 256), BF),
            pltpu.VMEM((2, XROWS, 256), BF),
            pltpu.VMEM((4, NB, XROWS, 256), BF),
            pltpu.VMEM((XROWS, 256), BF),
            pltpu.VMEM((2, NX, 2, 640, 256), BF),
            pltpu.VMEM((2, NX, 2, 256, 512), BF),
            pltpu.VMEM((NB, 10, 16, 256), BF),
            pltpu.VMEM((NB, QPAD, 640), BF),
            pltpu.VMEM((2, 2, QPAD, 640), BF),
            pltpu.VMEM((2, QPAD, 512), BF),
            pltpu.VMEM((NB, QPAD, 512), BF),
            pltpu.VMEM((NROWS, 512), BF),
            pltpu.VMEM((NROWS, 512), F32),
            pltpu.VMEM((NROWS, 128), F32),
            pltpu.VMEM((NROWS, 128), F32),
            pltpu.VMEM((NROWS, 256), F32),
            pltpu.VMEM((4, NB, NROWS, 256), BF),
            pltpu.VMEM((4, NB, NROWS, 256), BF),
            pltpu.VMEM((4, NB, NROWS, 256), BF),
            pltpu.VMEM((2, NROWS, 256), BF),
            dma((192,)),
            dma((2,)),
            dma,
            dma,
            dma((16,)),
            dma,
            dma((32,)),
            dma((32,)),
            dma,
            dma((4,)),
            dma((4,)),
            dma((16,)),
            dma((16,)),
            dma((2,)),
        ],
        compiler_params=pltpu.CompilerParams(
            collective_id=0, has_side_effects=True, vmem_limit_bytes=56 * 1024 * 1024
        ),
        name="decode_block",
    )(token_ids, lengths[None], table, gain, frequency, w_query, keyval, w_out, cache)
    return out.reshape(4, 40, 256)


def solution(mesh):
    in_specs = (
        P(None, "dp"),
        P("dp"),
        P(None, "tensor", "dp", None),
        P("tensor"),
        P("dp", "tensor"),
        P("dp", "tensor"),
        P("tensor", "dp"),
        P("dp", "tensor", None, None),
    )
    out_specs = P(None, "dp", "tensor")
    return jax.shard_map(body, mesh=mesh, in_specs=in_specs, out_specs=out_specs, check_vma=False)
```

```python
import functools
import math

import jax
import jax.numpy as jnp
import numpy as np
from jax import lax
from jax.experimental import pallas as pl
from jax.experimental.pallas import tpu as pltpu
from jax.sharding import PartitionSpec as P

EPS = 1e-06
THETA = 1000000.0
BF = jnp.bfloat16
F32 = jnp.float32

NX = 4
NZ = 8
NB = 4
QROWS = 40
QPAD = 48
NROWS = 160
XROWS = 176
HEAD = 128
FULL = 8192

MESH = pl.DeviceIdType.MESH


def kernel(
    tok_ref,
    len_ref,
    table_ref,
    gain_ref,
    freq_ref,
    wq_ref,
    wkv_ref,
    wo_ref,
    cache_ref,
    out_ref,
    tab,
    tokv,
    toks,
    lsend,
    cos_ref,
    sin_ref,
    lrecv,
    xt,
    xb,
    res,
    wbuf,
    wobuf,
    cbuf,
    qsend,
    qrecv,
    asend,
    arecv,
    att,
    qacc,
    kvacc,
    ssq,
    acc,
    sbuf,
    rright,
    rleft,
    frecv,
    send_sem,
    loc_sem,
    tok_sem,
    l_sem,
    x_sem,
    res_sem,
    w_sem,
    wo_sem,
    c_sem,
    q_sem,
    a_sem,
    rr_sem,
    rl_sem,
    f_sem,
):
    dp = lax.axis_index("dp")
    tn = lax.axis_index("tensor")
    x = dp // 4
    yh = (dp // 2) % 2
    c = dp % 2
    z = tn // 4
    b = tn % 4
    zpar = z % 2
    match = zpar == yh
    pair = b // 2
    bset = b % 2

    def dev(dp_, tn_):
        return {"dp": dp_, "tensor": tn_}

    def dpi(x_, yh_, c_):
        return (x_ * 2 + yh_) * 2 + c_

    pending = []
    counter = [0]

    def remote(src, dst, rsem, where, cond=None):
        n = counter[0]
        counter[0] += 1
        copy = pltpu.make_async_remote_copy(
            src_ref=src,
            dst_ref=dst,
            send_sem=send_sem.at[n],
            recv_sem=rsem,
            device_id=where,
            device_id_type=MESH,
        )
        if cond is None:
            copy.start()
        else:
            pl.when(cond)(copy.start)
        pending.append((cond, copy))

    def local(src, dst, sem, cond=None):
        copy = pltpu.make_async_copy(src, dst, sem)
        if cond is None:
            copy.start()
        else:
            pl.when(cond)(copy.start)

    def arrived(dst, sem):
        pltpu.make_async_copy(dst, dst, sem).wait()

    def to(src, dst, rsem, dp_, tn_):
        here = jnp.logical_and(dp_ == dp, tn_ == tn)
        remote(src, dst, rsem, dev(dp_, tn_), jnp.logical_not(here))
        local(src, dst, rsem, here)

    xr = (x + 1) % NX
    xl = (x + NX - 1) % NX
    xo = (x + 2) % NX
    zr = (z + 1) % NZ
    zl = (z + NZ - 1) % NZ
    right_z = dev(dp, zr * NB + b)
    left_z = dev(dp, zl * NB + b)

    table_copy = pltpu.make_async_copy(table_ref, tab, loc_sem.at[0])
    table_copy.start()
    own_shard = wbuf.at[bset, x, c]
    own_sem = w_sem.at[((bset * NX + x) * 2 + c) * 2]
    local(wq_ref, own_shard.at[pl.ds(0, 512)], own_sem)
    for h in (0, 1):
        local(
            wkv_ref.at[:, pl.ds(h * 256, 256)], own_shard.at[pl.ds(512 + h * 64, 64)], own_sem
        )

    barrier = pltpu.get_barrier_semaphore()
    partners = 0
    for i in range(1, 16):
        pl.semaphore_signal(barrier, inc=1, device_id=dev((dp + i) % 16, tn), device_id_type=MESH)
        partners += 1
    for i in range(1, 8):
        if i == 4:
            continue
        u = (yh * 4 + b + i) % 8
        pl.semaphore_signal(
            barrier, inc=1, device_id=dev(dpi(x, u // 4, c), z * NB + u % 4), device_id_type=MESH
        )
        partners += 1
    for where in (right_z, left_z):
        pl.semaphore_signal(barrier, inc=1, device_id=where, device_id_type=MESH)
        partners += 1

    pl.semaphore_wait(barrier, partners)

    for i in range(1, 16):
        remote(tok_ref, tokv.at[dp], tok_sem, dev((dp + i) % 16, tn))
    local(tok_ref, tokv.at[dp], tok_sem)

    class Gather:
        def __init__(self, buf, sem, half):
            self.buf, self.sem, self.half = buf, sem, half

        def slot(self, q, x_, c_, h=None):
            ref = self.buf.at[q, x_, c_]
            if h is None:
                return ref
            return ref.at[pl.ds(h * self.half, self.half)]

        def s(self, q, x_, c_, h=0):
            return self.sem.at[((q * NX + x_) * 2 + c_) * 2 + h]

        def send(self, src, q, x_, where):
            remote(src, self.slot(q, x_, c), self.s(q, x_, c), where)

        def first(self):
            own = (bset, x)
            src = self.slot(*own, c)
            arrived(src, self.s(*own, c))
            self.send(src, *own, dev(dp, z * NB + pair * 2 + 1 - bset))
            self.send(src, *own, dev(dpi(xr, yh, c), tn))
            self.send(src, *own, dev(dpi(xl, yh, c), tn))
            self.send(src, *own, dev(dpi(x, yh, 1 - c), tn))

        def second(self):
            q = 1 - bset
            arrived(self.slot(q, x, c), self.s(q, x, c))
            src = self.slot(q, x, c)
            self.send(src, q, x, dev(dpi(xr, yh, c), tn))
            self.send(src, q, x, dev(dpi(xl, yh, c), tn))
            self.send(src, q, x, dev(dpi(x, yh, 1 - c), tn))

        def relay(self, q):
            for x_, h, to_x in ((xl, 0, xr), (xr, 1, xl)):
                arrived(self.slot(q, x_, c), self.s(q, x_, c))
                remote(
                    self.slot(q, x_, c, h),
                    self.slot(q, x_, c, h),
                    self.s(q, x_, c, h),
                    dev(dpi(to_x, yh, c), tn),
                )
                self.send(self.slot(q, x_, c), q, x_, dev(dpi(x, yh, 1 - c), tn))

        def last(self, q):
            for h in (0, 1):
                arrived(self.slot(q, xo, c, h), self.s(q, xo, c, h))
            self.send(self.slot(q, xo, c), q, xo, dev(dpi(x, yh, 1 - c), tn))

        def finish(self):
            for q in (0, 1):
                for x_ in range(NX):
                    arrived(self.slot(q, x_, 1 - c), self.s(q, x_, 1 - c))

    wqkv = Gather(wbuf, w_sem, 320)
    wout = Gather(wobuf, wo_sem, 128)
    wqkv.first()
    local(wo_ref, wout.slot(bset, x, c), wout.s(bset, x, c))

    arrived(tokv, tok_sem)
    to_scalar = pltpu.make_async_copy(tokv, toks, loc_sem.at[1])
    to_scalar.start()
    to_scalar.wait()
    table_copy.wait()

    lane = lax.broadcasted_iota(jnp.int32, (16, 128), 1)
    wide = lax.broadcasted_iota(jnp.int32, (16, 256), 1)
    feature = lax.broadcasted_iota(jnp.int32, (16, 256), 0)
    gain_column = jnp.sum(
        jnp.where(wide == dp * 16 + feature, gain_ref[...].astype(F32)[None], 0.0),
        axis=1,
        keepdims=True,
    )
    gain_tail = jnp.where(lane == NROWS - 128, gain_column, 0.0)
    place = x * 2 + c
    lookup_base = counter[0]
    counter[0] += 8

    def lookup_copy(e):
        dp2 = dpi(e // 2, zpar, e % 2)
        return dp2, pltpu.make_async_remote_copy(
            src_ref=lsend.at[e],
            dst_ref=lrecv.at[dp],
            send_sem=send_sem.at[lookup_base + e],
            recv_sem=l_sem,
            device_id=dev(dp2, tn),
            device_id_type=MESH,
        )

    def lookup(i, carry):
        e = (place + 1 + i) % 8

        def one_set(s, carry):
            d2 = dpi(e // 2, s, e % 2)
            for half, count in ((0, 128), (1, NROWS - 128)):
                found = jnp.zeros((16, 128), F32) if half == 0 else gain_tail
                for n in range(count):
                    row = half * 128 + n
                    token = toks[d2, row % 4, row // 4]
                    block = lax.shift_right_logical(token, 7)
                    tile = tab[:, pl.ds(block * 128, 128)].astype(F32)
                    picked = jnp.where(lane == jnp.bitwise_and(token, 127), tile, 0.0)
                    found = jnp.where(lane == n, jnp.sum(picked, axis=1, keepdims=True), found)
                lsend[e, s, :, pl.ds(half * 128, 128)] = found.astype(BF)
            return carry

        lax.fori_loop(0, 2, one_set, 0)
        dp2, copy = lookup_copy(e)
        pl.when(dp2 != dp)(copy.start)
        pl.when(dp2 == dp)(pltpu.make_async_copy(lsend.at[e], lrecv.at[dp], l_sem).start)
        return carry

    lax.fori_loop(0, 4, lookup, 0)
    wqkv.second()
    wqkv.relay(bset)
    lax.fori_loop(4, 8, lookup, 0)

    k_here = z // 2

    pl.when(match)(lambda: arrived(lrecv, l_sem))
    for s in (0, 1):

        @pl.when(match)
        def _(s=s):
            features = lrecv[:, s].reshape(256, 256).astype(F32)
            xt[s] = features.T[:XROWS].astype(BF)

        for h in (0, 1):
            b2 = s + 2 * h
            here = b2 == b
            dst = xb.at[k_here, b]
            sem = x_sem.at[k_here * NB + b]
            remote(
                xt.at[s],
                dst,
                sem,
                dev(dp, z * NB + b2),
                jnp.logical_and(match, jnp.logical_not(here)),
            )
            local(xt.at[s], dst, sem, jnp.logical_and(match, here))

    def by_b(values):
        return jnp.where(
            b == 0, values[0], jnp.where(b == 1, values[1], jnp.where(b == 2, values[2], values[3]))
        )

    nearest = [by_b(v) for v in ((0, 1, 2, 3), (1, 0, 3, 2), (2, 2, 1, 1), (3, 3, 0, 0))]
    if_match = [(0, i) for i in range(4)]
    if_match += [(d, i) for i in range(4) for d in (2, 6)]
    if_match += [(4, i) for i in range(4)]
    if_not = [(d, i) for i in range(4) for d in (1, 7)]
    if_not += [(d, i) for i in range(4) for d in (3, 5)]
    blocks = []
    for (d_m, i_m), (d_n, i_n) in zip(if_match, if_not):
        delta = jnp.where(match, d_m, d_n)
        b_ = jnp.where(match, nearest[i_m], nearest[i_n])
        blocks.append((delta, ((z - delta + NZ) % NZ) // 2, b_))

    row40 = lax.broadcasted_iota(jnp.int32, (QROWS, 128), 0)
    lane40 = lax.broadcasted_iota(jnp.int32, (QROWS, 128), 1)

    def angles():
        lengths = len_ref[...].astype(F32)
        row_of = lax.broadcasted_iota(jnp.int32, (QROWS, 40), 0) // 4 + b * 10
        all_rows = lax.broadcasted_iota(jnp.int32, (QROWS, 40), 1)
        length = jnp.sum(jnp.where(all_rows == row_of, lengths, 0.0), axis=1, keepdims=True)
        turn = (length + (row40 % 4).astype(F32)) * freq_ref[...]
        cos_ref[...] = jnp.cos(turn)
        sin_ref[...] = jnp.where(lane40 < HEAD // 2, -1.0, 1.0) * jnp.sin(turn)
        return length

    def forward(n):
        delta, k, b_ = blocks[n]
        reach = jnp.where(b_ < 2, 4, 3)
        block = xb.at[k, b_]
        sem = x_sem.at[k * NB + b_]
        arrived(block, sem)
        if n < 4:
            onward = delta == 0
        else:
            onward = False
        onward = jnp.logical_or(
            onward, jnp.logical_and(delta > reach, 8 - delta < 7 - reach)
        )
        remote(block, block, sem, right_z, delta < reach)
        remote(block, block, sem, left_z, onward)

    def project(n):
        _, k, b_ = blocks[n]
        c_ = b_ // 2
        h = b_ % 2
        raw = xb[k, b_].astype(F32)
        rows = raw[:NROWS]
        gain = raw[NROWS : NROWS + 1]
        scaled = (rows * gain).astype(BF)
        square = rows * rows
        square = square[:, :128] + square[:, 128:]
        parts = [
            jnp.dot(scaled, wbuf[q, k, c_, pl.ds(h * 256, 256)], preferred_element_type=F32)
            for q in (0, 1)
        ]
        keyval = jnp.concatenate(
            [wbuf[q, k, c_, pl.ds(512 + h * 64, 64)] for q in (0, 1)], axis=0
        )
        kv = lax.dot_general(
            scaled, keyval, (((1,), (1,)), ((), ())), preferred_element_type=F32
        )
        if n == 0:
            ssq[...] = square
            qacc[:, :256] = parts[0]
            qacc[:, 256:] = parts[1]
            kvacc[...] = kv
        else:
            ssq[...] += square
            qacc[:, :256] += parts[0]
            qacc[:, 256:] += parts[1]
            kvacc[...] += kv

    forward(0)
    wqkv.relay(1 - bset)
    forward(1)
    wqkv.last(bset)
    forward(2)
    forward(3)
    wqkv.last(1 - bset)
    for n in range(4, 16):
        forward(n)
        if n == 4:
            wout.first()
            length = angles()
        if n == 6:
            for i in range(NB):
                b2 = (b + i) % NB
                to(cache_ref.at[pl.ds(b2 * 10, 10)], cbuf.at[b], c_sem, dp, z * NB + b2)
        if n == 8:
            for_partner = 1 - zpar
            remote(xt.at[for_partner], res, res_sem, dev(dpi(x, for_partner, c), tn), match)
            local(xt.at[yh], res, res_sem, match)
        if n == 9:
            wout.second()
        if n == 14:
            wout.relay(bset)
        if n == 7:
            wqkv.finish()
        if n >= 7:
            for m in range(2 * (n - 7), min(2 * (n - 7) + 2, n + 1)):
                project(m)
    project(15)

    diagonal = row40 == lane40
    row8 = lax.broadcasted_iota(jnp.int32, (8, 128), 0)
    for i in range(NB):
        total = jnp.sum(ssq[i * QROWS : (i + 1) * QROWS], axis=1, keepdims=True)
        flat = jnp.sum(jnp.where(diagonal, total, 0.0), axis=0, keepdims=True)
        high = flat.astype(BF).astype(F32)
        low = flat - high
        tail = jnp.where(row8 == 0, high, jnp.where(row8 == 1, low, 0.0))
        tail = jnp.concatenate([tail, jnp.zeros((8, 512), F32)], axis=1)
        body_rows = jnp.concatenate(
            [qacc[i * QROWS : (i + 1) * QROWS], kvacc[i * QROWS : (i + 1) * QROWS]], axis=1
        )
        qsend[i] = jnp.concatenate([body_rows, tail], axis=0).astype(BF)
        to(
            qsend.at[i],
            qrecv.at[yh, pair],
            q_sem.at[yh * 2 + pair],
            dpi(x, bset, c),
            z * NB + i,
        )

    wout.relay(1 - bset)

    for i in range(NB):
        arrived(qrecv.at[i // 2, i % 2], q_sem.at[i])
    arrived(cbuf, c_sem)

    tails = qrecv[0, 0, 32:QPAD, :128].astype(F32) + qrecv[1, 0, 32:QPAD, :128].astype(F32)
    flat = tails[8:9] + tails[9:10]
    total = jnp.sum(jnp.where(diagonal, flat, 0.0), axis=1, keepdims=True)
    factor = lax.rsqrt(total * (1.0 / FULL) + EPS)
    cosine = cos_ref[...]
    sine = sin_ref[...]

    def rope(u):
        return u * cosine + pltpu.roll(u, HEAD // 2, 1) * sine

    heads = []
    news = []
    for p in (0, 1):
        both = qrecv[0, p].astype(F32) + qrecv[1, p].astype(F32)
        both = both[:QROWS] * factor
        for i in range(4):
            heads.append(rope(both[:, i * HEAD : (i + 1) * HEAD]))
        news.append(both[:, 512:640])
    query = jnp.concatenate(heads, axis=0).astype(BF)
    no_rows = jnp.zeros((128 - QROWS, HEAD), F32)
    key_new = rope(news[0].astype(BF).astype(F32))
    key_new = jnp.concatenate([key_new, no_rows], axis=0).astype(BF)
    value_new = jnp.concatenate([news[1], no_rows], axis=0).astype(BF)
    keys = cbuf[:, :, :, :HEAD].reshape(640, HEAD)
    values = cbuf[:, :, :, HEAD:].reshape(640, HEAD)

    contract_last = (((1,), (1,)), ((), ()))
    inv_root = 1.0 / math.sqrt(HEAD)
    scores_old = lax.dot_general(query, keys, contract_last, preferred_element_type=F32) * inv_root
    scores_new = (
        lax.dot_general(query, key_new, contract_last, preferred_element_type=F32) * inv_root
    )
    col = lax.broadcasted_iota(jnp.int32, (QROWS, 640), 1)
    row = lax.broadcasted_iota(jnp.int32, (QROWS, 640), 0) // 4
    within = col % 160
    position = (col // 160) * 16 + within % 16
    old_ok = jnp.logical_and(within // 16 == row, position.astype(F32) < length)
    new_ok = jnp.logical_and(
        lane40 // 4 == row40 // 4, jnp.logical_and(lane40 <= row40, lane40 < QROWS)
    )
    old_bias = jnp.where(old_ok, 0.0, -1e30)
    new_bias = jnp.where(new_ok, 0.0, -1e30)
    old_bias = jnp.concatenate([old_bias] * 8, axis=0)
    new_bias = jnp.concatenate([new_bias] * 8, axis=0)
    scores_old = jnp.where(old_bias == 0.0, scores_old, -1e30)
    scores_new = jnp.where(new_bias == 0.0, scores_new, -1e30)
    top = jnp.maximum(
        jnp.max(scores_old, axis=1, keepdims=True), jnp.max(scores_new, axis=1, keepdims=True)
    )
    exp_old = jnp.exp(scores_old - top)
    exp_new = jnp.exp(scores_new - top)
    totals = jnp.sum(exp_old, axis=1, keepdims=True) + jnp.sum(exp_new, axis=1, keepdims=True)
    probs_old = (exp_old / totals).astype(BF)
    probs_new = (exp_new / totals).astype(BF)
    attended = jnp.dot(probs_old, values, preferred_element_type=F32)
    attended = attended + jnp.dot(probs_new, value_new, preferred_element_type=F32)
    for p in (0, 1):
        side = jnp.concatenate(
            [attended[(4 * p + i) * QROWS : (4 * p + i + 1) * QROWS] for i in range(4)], axis=1
        )
        asend[p] = jnp.concatenate([side, jnp.zeros((QPAD - QROWS, 512), F32)], axis=0).astype(BF)
        for y_ in (0, 1):
            to(asend.at[p], arecv.at[b], a_sem.at[b], dpi(x, y_, c), z * NB + p * 2 + yh)

    wout.last(bset)
    wout.last(1 - bset)
    wout.finish()
    for i in range(NB):
        arrived(arecv.at[i], a_sem.at[i])
    att[...] = jnp.concatenate(
        [arecv[i].astype(F32)[:QROWS] for i in range(NB)], axis=0
    ).astype(BF)

    cross = ((2, 0), (3, 1), (0, 2), (1, 3))
    if_match = [(4, i) for i in range(4)]
    if_match += [item for i, j in cross for item in ((2, i), (6, j))]
    if_match += [(0, i) for i in (2, 0, 3, 1)]
    if_not = [item for i, j in cross for item in ((3, i), (5, j))]
    if_not += [item for i, j in cross for item in ((1, i), (7, j))]
    for n in range(16):
        (d_m, i_m), (d_n, i_n) = if_match[n], if_not[n]
        delta = jnp.where(match, d_m, d_n)
        b_ = jnp.where(match, i_m, i_n)
        k = ((z + delta) % NZ) // 2
        reach = jnp.where(b_ < 2, 4, 3)
        is_end = delta == 0
        c_ = b_ // 2
        h = b_ % 2
        part = jnp.dot(
            att[:, :256], wobuf[0, k, c_, :, pl.ds(h * 256, 256)], preferred_element_type=F32
        )
        acc[...] = part + jnp.dot(
            att[:, 256:], wobuf[1, k, c_, :, pl.ds(h * 256, 256)], preferred_element_type=F32
        )
        from_left = delta + 1 <= reach
        from_right = jnp.logical_or(delta > reach + 1, is_end)
        index = k * NB + b_

        @pl.when(from_left)
        def _(index=index, k=k, b_=b_):
            arrived(rright.at[k, b_], rr_sem.at[index])
            acc[...] += rright[k, b_].astype(F32)

        @pl.when(from_right)
        def _(index=index, k=k, b_=b_):
            arrived(rleft.at[k, b_], rl_sem.at[index])
            acc[...] += rleft[k, b_].astype(F32)

        src = sbuf.at[k, b_]
        src[...] = acc[...].astype(BF)
        remote(
            src,
            rright.at[k, b_],
            rr_sem.at[index],
            right_z,
            jnp.logical_and(delta >= 1, delta <= reach),
        )
        remote(src, rleft.at[k, b_], rl_sem.at[index], left_z, delta > reach)
        if n >= 12:
            dp_ = dpi(x, bset, c)
            tn_ = z * NB + b_
            here = jnp.logical_and(dp_ == dp, tn_ == tn)
            remote(
                src,
                frecv.at[pair],
                f_sem.at[pair],
                dev(dp_, tn_),
                jnp.logical_and(is_end, jnp.logical_not(here)),
            )
            local(src, frecv.at[pair], f_sem.at[pair], jnp.logical_and(is_end, here))

    arrived(res, res_sem)
    for p in (0, 1):
        arrived(frecv.at[p], f_sem.at[p])
    hidden = res[:NROWS].astype(F32) + (frecv[0].astype(F32) + frecv[1].astype(F32))
    hidden = jnp.concatenate([hidden, jnp.zeros((256 - NROWS, 256), F32)], axis=0).astype(BF)
    to_row = lax.broadcasted_iota(jnp.int32, (NROWS, 256), 0)
    from_row = lax.broadcasted_iota(jnp.int32, (NROWS, 256), 1)
    order = jnp.where(from_row == (to_row % 40) * 4 + to_row // 40, 1.0, 0.0).astype(BF)
    out_ref[...] = jnp.dot(order, hidden, preferred_element_type=F32).astype(BF)

    for cond, copy in pending:
        if cond is None:
            copy.wait_send()
        else:
            pl.when(cond)(copy.wait_send)

    def lookup_sent(e, carry):
        dp2, copy = lookup_copy(e)
        pl.when(dp2 != dp)(copy.wait_send)
        return carry

    lax.fori_loop(0, 8, lookup_sent, 0)


def body(
    token_ids, lengths, embed_table, norm_gain, w_query, key_value_weight, w_out, key_value_cache
):
    table = embed_table.reshape(16, -1)
    frequency = THETA ** (-(np.arange(64) / 64))
    frequency = jnp.asarray(np.concatenate([frequency, frequency])[None], F32)
    keyval = key_value_weight.T
    cache = key_value_cache.reshape(40, 16, 256)

    vmem = pl.BlockSpec(memory_space=pltpu.VMEM)
    anywhere = pl.BlockSpec(memory_space=pl.ANY)
    dma = pltpu.SemaphoreType.DMA
    out = pl.pallas_call(
        kernel,
        out_shape=jax.ShapeDtypeStruct((NROWS, 256), BF),
        in_specs=[vmem, vmem, anywhere, vmem, vmem, anywhere, anywhere, anywhere, anywhere],
        out_specs=vmem,
        scratch_shapes=[
            pltpu.VMEM((16, 81920), BF),
            pltpu.VMEM((16, 4, 40), jnp.int32),
            pltpu.SMEM((16, 4, 40), jnp.int32),
            pltpu.VMEM((8, 2, 16, 256), BF),
            pltpu.VMEM((QROWS, HEAD), F32),
            pltpu.VMEM((QROWS, HEAD), F32),
            pltpu.VMEM((16, 2, 16, 256), BF),
            pltpu.VMEM((2, XROWS, 256), BF),
            pltpu.VMEM((4, NB, XROWS, 256), BF),
            pltpu.VMEM((XROWS, 256), BF),
            pltpu.VMEM((2, NX, 2, 640, 256), BF),
            pltpu.VMEM((2, NX, 2, 256, 512), BF),
            pltpu.VMEM((NB, 10, 16, 256), BF),
            pltpu.VMEM((NB, QPAD, 640), BF),
            pltpu.VMEM((2, 2, QPAD, 640), BF),
            pltpu.VMEM((2, QPAD, 512), BF),
            pltpu.VMEM((NB, QPAD, 512), BF),
            pltpu.VMEM((NROWS, 512), BF),
            pltpu.VMEM((NROWS, 512), F32),
            pltpu.VMEM((NROWS, 128), F32),
            pltpu.VMEM((NROWS, 128), F32),
            pltpu.VMEM((NROWS, 256), F32),
            pltpu.VMEM((4, NB, NROWS, 256), BF),
            pltpu.VMEM((4, NB, NROWS, 256), BF),
            pltpu.VMEM((4, NB, NROWS, 256), BF),
            pltpu.VMEM((2, NROWS, 256), BF),
            dma((192,)),
            dma((2,)),
            dma,
            dma,
            dma((16,)),
            dma,
            dma((32,)),
            dma((32,)),
            dma,
            dma((4,)),
            dma((4,)),
            dma((16,)),
            dma((16,)),
            dma((2,)),
        ],
        compiler_params=pltpu.CompilerParams(
            collective_id=0, has_side_effects=True, vmem_limit_bytes=56 * 1024 * 1024
        ),
        name="decode_block",
    )(token_ids, lengths[None], table, norm_gain, frequency, w_query, keyval, w_out, cache)
    return out.reshape(4, 40, 256)


def solution(mesh):
    in_specs = (
        P(None, "dp"),
        P("dp"),
        P(None, "tensor", "dp", None),
        P("tensor"),
        P("dp", "tensor"),
        P("dp", "tensor"),
        P("tensor", "dp"),
        P("dp", "tensor", None, None),
    )
    out_specs = P(None, "dp", "tensor")
    return jax.shard_map(body, mesh=mesh, in_specs=in_specs, out_specs=out_specs, check_vma=False)
```

```python
import functools
import math

import jax
import jax.numpy as jnp
import numpy as np
from jax import lax
from jax.experimental import pallas as pl
from jax.experimental.pallas import tpu as pltpu
from jax.sharding import PartitionSpec as P

EPS = 1e-06
THETA = 1000000.0
BF = jnp.bfloat16
F32 = jnp.float32

NX = 4
NZ = 8
NB = 4
QROWS = 40
QPAD = 48
NROWS = 160
XROWS = 176
HEAD = 128
FULL = 8192

MESH = pl.DeviceIdType.MESH


def kernel(
    tok_ref,
    len_ref,
    table_ref,
    gain_ref,
    freq_ref,
    wq_ref,
    wkv_ref,
    wo_ref,
    cache_ref,
    out_ref,
    tab,
    tokv,
    toks,
    lsend,
    cos_ref,
    sin_ref,
    lrecv,
    xt,
    xb,
    wbuf,
    wobuf,
    cbuf,
    qsend,
    qrecv,
    asend,
    arecv,
    att,
    qacc,
    kvacc,
    ssq,
    acc,
    sbuf,
    rright,
    rleft,
    frecv,
    send_sem,
    loc_sem,
    tok_sem,
    l_sem,
    x_sem,
    w_sem,
    wo_sem,
    c_sem,
    q_sem,
    a_sem,
    rr_sem,
    rl_sem,
    f_sem,
):
    dp = lax.axis_index("dp")
    tn = lax.axis_index("tensor")
    x = dp // 4
    yh = (dp // 2) % 2
    c = dp % 2
    z = tn // 4
    b = tn % 4
    zpar = z % 2
    match = zpar == yh
    pair = b // 2
    bset = b % 2

    def dev(dp_, tn_):
        return {"dp": dp_, "tensor": tn_}

    def dpi(x_, yh_, c_):
        return (x_ * 2 + yh_) * 2 + c_

    pending = []
    counter = [0]

    def remote(src, dst, rsem, where, cond=None):
        n = counter[0]
        counter[0] += 1
        copy = pltpu.make_async_remote_copy(
            src_ref=src,
            dst_ref=dst,
            send_sem=send_sem.at[n],
            recv_sem=rsem,
            device_id=where,
            device_id_type=MESH,
        )
        if cond is None:
            copy.start()
        else:
            pl.when(cond)(copy.start)
        pending.append((cond, copy))

    def local(src, dst, sem, cond=None):
        copy = pltpu.make_async_copy(src, dst, sem)
        if cond is None:
            copy.start()
        else:
            pl.when(cond)(copy.start)

    def arrived(dst, sem):
        pltpu.make_async_copy(dst, dst, sem).wait()

    def to(src, dst, rsem, dp_, tn_):
        here = jnp.logical_and(dp_ == dp, tn_ == tn)
        remote(src, dst, rsem, dev(dp_, tn_), jnp.logical_not(here))
        local(src, dst, rsem, here)

    xr = (x + 1) % NX
    xl = (x + NX - 1) % NX
    xo = (x + 2) % NX
    zr = (z + 1) % NZ
    zl = (z + NZ - 1) % NZ
    right_z = dev(dp, zr * NB + b)
    left_z = dev(dp, zl * NB + b)

    table_copy = pltpu.make_async_copy(table_ref, tab, loc_sem.at[0])
    table_copy.start()
    local(tok_ref, tokv.at[dp], tok_sem.at[dp])
    own_shard = wbuf.at[bset, x, c]
    own_sem = w_sem.at[((bset * NX + x) * 2 + c) * 2]
    local(wq_ref, own_shard.at[pl.ds(0, 512)], own_sem)
    for h in (0, 1):
        local(
            wkv_ref.at[:, pl.ds(h * 256, 256)], own_shard.at[pl.ds(512 + h * 64, 64)], own_sem
        )

    barrier = pltpu.get_barrier_semaphore()
    partners = 0
    for i in range(1, 16):
        pl.semaphore_signal(barrier, inc=1, device_id=dev((dp + i) % 16, tn), device_id_type=MESH)
        partners += 1
    for i in range(1, 8):
        if i == 4:
            continue
        u = (yh * 4 + b + i) % 8
        pl.semaphore_signal(
            barrier, inc=1, device_id=dev(dpi(x, u // 4, c), z * NB + u % 4), device_id_type=MESH
        )
        partners += 1
    for where in (right_z, left_z):
        pl.semaphore_signal(barrier, inc=1, device_id=where, device_id_type=MESH)
        partners += 1

    pl.semaphore_wait(barrier, partners)

    for i in range(1, 16):
        remote(tok_ref, tokv.at[dp], tok_sem.at[dp], dev((dp + i) % 16, tn))

    class Gather:
        def __init__(self, buf, sem, half):
            self.buf, self.sem, self.half = buf, sem, half

        def slot(self, q, x_, c_, h=None):
            ref = self.buf.at[q, x_, c_]
            if h is None:
                return ref
            return ref.at[pl.ds(h * self.half, self.half)]

        def s(self, q, x_, c_, h=0):
            return self.sem.at[((q * NX + x_) * 2 + c_) * 2 + h]

        def send(self, src, q, x_, where):
            remote(src, self.slot(q, x_, c), self.s(q, x_, c), where)

        def to_pair(self):
            own = (bset, x)
            src = self.slot(*own, c)
            arrived(src, self.s(*own, c))
            self.send(src, *own, dev(dp, z * NB + pair * 2 + 1 - bset))

        def first(self):
            own = (bset, x)
            src = self.slot(*own, c)
            self.send(src, *own, dev(dpi(xr, yh, c), tn))
            self.send(src, *own, dev(dpi(xl, yh, c), tn))
            self.send(src, *own, dev(dpi(x, yh, 1 - c), tn))

        def second(self):
            q = 1 - bset
            arrived(self.slot(q, x, c), self.s(q, x, c))
            src = self.slot(q, x, c)
            self.send(src, q, x, dev(dpi(xr, yh, c), tn))
            self.send(src, q, x, dev(dpi(xl, yh, c), tn))
            self.send(src, q, x, dev(dpi(x, yh, 1 - c), tn))

        def relay(self, q):
            for x_, h, to_x in ((xl, 0, xr), (xr, 1, xl)):
                arrived(self.slot(q, x_, c), self.s(q, x_, c))
                remote(
                    self.slot(q, x_, c, h),
                    self.slot(q, x_, c, h),
                    self.s(q, x_, c, h),
                    dev(dpi(to_x, yh, c), tn),
                )
                self.send(self.slot(q, x_, c), q, x_, dev(dpi(x, yh, 1 - c), tn))

        def last(self, q):
            for h in (0, 1):
                arrived(self.slot(q, xo, c, h), self.s(q, xo, c, h))
            self.send(self.slot(q, xo, c), q, xo, dev(dpi(x, yh, 1 - c), tn))

        def finish(self):
            for q in (0, 1):
                for x_ in range(NX):
                    arrived(self.slot(q, x_, 1 - c), self.s(q, x_, 1 - c))

    wqkv = Gather(wbuf, w_sem, 320)
    wout = Gather(wobuf, wo_sem, 128)
    wqkv.to_pair()
    wqkv.first()
    local(wo_ref, wout.slot(bset, x, c), wout.s(bset, x, c))

    place = x * 2 + c

    def source(i):
        e = (place + i % 8) % 8
        s = (yh + i // 8) % 2
        return e, s, dpi(e // 2, s, e % 2)

    def to_scalar(i):
        _, _, d2 = source(i)
        return pltpu.make_async_copy(tokv.at[d2], toks.at[d2], loc_sem.at[1 + i % 2])

    def fetch(i):
        _, _, d2 = source(i)
        arrived(tokv.at[d2], tok_sem.at[d2])
        to_scalar(i).start()

    fetch(0)
    table_copy.wait()

    lane = lax.broadcasted_iota(jnp.int32, (16, 128), 1)
    wide = lax.broadcasted_iota(jnp.int32, (16, 256), 1)
    feature = lax.broadcasted_iota(jnp.int32, (16, 256), 0)
    gain_column = jnp.sum(
        jnp.where(wide == dp * 16 + feature, gain_ref[...].astype(F32)[None], 0.0),
        axis=1,
        keepdims=True,
    )
    gain_tail = jnp.where(lane == NROWS - 128, gain_column, 0.0)
    lookup_base = counter[0]
    counter[0] += 8

    def lookup_copy(e):
        dp2 = dpi(e // 2, zpar, e % 2)
        return dp2, pltpu.make_async_remote_copy(
            src_ref=lsend.at[e],
            dst_ref=lrecv.at[dp],
            send_sem=send_sem.at[lookup_base + e],
            recv_sem=l_sem,
            device_id=dev(dp2, tn),
            device_id_type=MESH,
        )

    def lookup(i, carry):
        e, s, d2 = source(i)
        pl.when(i < 15)(lambda: fetch(i + 1))
        to_scalar(i).wait()
        for half, count in ((0, 128), (1, NROWS - 128)):
            found = jnp.zeros((16, 128), F32) if half == 0 else gain_tail
            for n in range(count):
                row = half * 128 + n
                token = toks[d2, row % 4, row // 4]
                block = lax.shift_right_logical(token, 7)
                tile = tab[:, pl.ds(block * 128, 128)].astype(F32)
                picked = jnp.where(lane == jnp.bitwise_and(token, 127), tile, 0.0)
                found = jnp.where(lane == n, jnp.sum(picked, axis=1, keepdims=True), found)
            lsend[e, s, :, pl.ds(half * 128, 128)] = found.astype(BF)

        @pl.when(i >= 8)
        def _():
            dp2, copy = lookup_copy(e)
            pl.when(dp2 != dp)(copy.start)
            pl.when(dp2 == dp)(pltpu.make_async_copy(lsend.at[e], lrecv.at[dp], l_sem).start)

        return carry

    lax.fori_loop(0, 16, lookup, 0)
    wqkv.second()
    wqkv.relay(bset)

    k_here = z // 2

    pl.when(match)(lambda: arrived(lrecv, l_sem))
    for s in (0, 1):

        @pl.when(match)
        def _(s=s):
            features = lrecv[:, s].reshape(256, 256).astype(F32)
            xt[s] = features.T[:XROWS].astype(BF)

        for h in (0, 1):
            b2 = s + 2 * h
            here = b2 == b
            dst = xb.at[k_here, b]
            sem = x_sem.at[k_here * NB + b]
            remote(
                xt.at[s],
                dst,
                sem,
                dev(dp, z * NB + b2),
                jnp.logical_and(match, jnp.logical_not(here)),
            )
            local(xt.at[s], dst, sem, jnp.logical_and(match, here))

    def by_b(values):
        return jnp.where(
            b == 0, values[0], jnp.where(b == 1, values[1], jnp.where(b == 2, values[2], values[3]))
        )

    nearest = [by_b(v) for v in ((0, 1, 2, 3), (1, 0, 3, 2), (2, 2, 1, 1), (3, 3, 0, 0))]
    if_match = [(0, i) for i in range(4)]
    if_match += [(d, i) for i in range(4) for d in (2, 6)]
    if_match += [(4, i) for i in range(4)]
    if_not = [(d, i) for i in range(4) for d in (1, 7)]
    if_not += [(d, i) for i in range(4) for d in (3, 5)]
    blocks = []
    for (d_m, i_m), (d_n, i_n) in zip(if_match, if_not):
        delta = jnp.where(match, d_m, d_n)
        b_ = jnp.where(match, nearest[i_m], nearest[i_n])
        blocks.append((delta, ((z - delta + NZ) % NZ) // 2, b_))

    row40 = lax.broadcasted_iota(jnp.int32, (QROWS, 128), 0)
    lane40 = lax.broadcasted_iota(jnp.int32, (QROWS, 128), 1)

    def angles():
        lengths = len_ref[...].astype(F32)
        row_of = lax.broadcasted_iota(jnp.int32, (QROWS, 40), 0) // 4 + b * 10
        all_rows = lax.broadcasted_iota(jnp.int32, (QROWS, 40), 1)
        length = jnp.sum(jnp.where(all_rows == row_of, lengths, 0.0), axis=1, keepdims=True)
        turn = (length + (row40 % 4).astype(F32)) * freq_ref[...]
        cos_ref[...] = jnp.cos(turn)
        sin_ref[...] = jnp.where(lane40 < HEAD // 2, -1.0, 1.0) * jnp.sin(turn)
        return length

    def forward(n):
        delta, k, b_ = blocks[n]
        reach = jnp.where(b_ < 2, 4, 3)
        block = xb.at[k, b_]
        sem = x_sem.at[k * NB + b_]
        arrived(block, sem)
        if n < 4:
            onward = delta == 0
        else:
            onward = False
        onward = jnp.logical_or(
            onward, jnp.logical_and(delta > reach, 8 - delta < 7 - reach)
        )
        remote(block, block, sem, right_z, delta < reach)
        remote(block, block, sem, left_z, onward)

    def project(n):
        _, k, b_ = blocks[n]
        c_ = b_ // 2
        h = b_ % 2
        raw = xb[k, b_].astype(F32)
        rows = raw[:NROWS]
        gain = raw[NROWS : NROWS + 1]
        scaled = (rows * gain).astype(BF)
        square = rows * rows
        square = square[:, :128] + square[:, 128:]
        parts = [
            jnp.dot(scaled, wbuf[q, k, c_, pl.ds(h * 256, 256)], preferred_element_type=F32)
            for q in (0, 1)
        ]
        keyval = jnp.concatenate(
            [wbuf[q, k, c_, pl.ds(512 + h * 64, 64)] for q in (0, 1)], axis=0
        )
        kv = lax.dot_general(
            scaled, keyval, (((1,), (1,)), ((), ())), preferred_element_type=F32
        )
        if n == 0:
            ssq[...] = square
            qacc[:, :256] = parts[0]
            qacc[:, 256:] = parts[1]
            kvacc[...] = kv
        else:
            ssq[...] += square
            qacc[:, :256] += parts[0]
            qacc[:, 256:] += parts[1]
            kvacc[...] += kv

    forward(0)
    wqkv.relay(1 - bset)
    forward(1)
    wqkv.last(bset)
    forward(2)
    forward(3)
    wout.to_pair()
    wqkv.last(1 - bset)
    for n in range(4, 16):
        forward(n)
        if n == 5:
            wout.first()
        if n == 8:
            for i in range(NB):
                b2 = (b + i) % NB
                to(cache_ref.at[pl.ds(b2 * 10, 10)], cbuf.at[b], c_sem, dp, z * NB + b2)
        if n == 9:
            wout.second()
        if n == 11:
            wqkv.finish()
            for m in range(11):
                project(m)
        if n >= 11:
            project(n)
        if n == 14:
            wout.relay(bset)

    diagonal = row40 == lane40
    row8 = lax.broadcasted_iota(jnp.int32, (8, 128), 0)
    for i in range(NB):
        total = jnp.sum(ssq[i * QROWS : (i + 1) * QROWS], axis=1, keepdims=True)
        flat = jnp.sum(jnp.where(diagonal, total, 0.0), axis=0, keepdims=True)
        high = flat.astype(BF).astype(F32)
        low = flat - high
        tail = jnp.where(row8 == 0, high, jnp.where(row8 == 1, low, 0.0))
        tail = jnp.concatenate([tail, jnp.zeros((8, 512), F32)], axis=1)
        body_rows = jnp.concatenate(
            [qacc[i * QROWS : (i + 1) * QROWS], kvacc[i * QROWS : (i + 1) * QROWS]], axis=1
        )
        qsend[i] = jnp.concatenate([body_rows, tail], axis=0).astype(BF)
        to(
            qsend.at[i],
            qrecv.at[yh, pair],
            q_sem.at[yh * 2 + pair],
            dpi(x, bset, c),
            z * NB + i,
        )

    wout.relay(1 - bset)

    length = angles()
    col = lax.broadcasted_iota(jnp.int32, (QROWS, 640), 1)
    row = lax.broadcasted_iota(jnp.int32, (QROWS, 640), 0) // 4
    within = col % 160
    position = (col // 160) * 16 + within % 16
    old_ok = jnp.logical_and(within // 16 == row, position.astype(F32) < length)
    new_ok = jnp.logical_and(
        lane40 // 4 == row40 // 4, jnp.logical_and(lane40 <= row40, lane40 < QROWS)
    )
    old_bias = jnp.where(old_ok, 0.0, -1e30)
    new_bias = jnp.where(new_ok, 0.0, -1e30)
    old_bias = jnp.concatenate([old_bias] * 8, axis=0)
    new_bias = jnp.concatenate([new_bias] * 8, axis=0)
    for i in range(NB):
        arrived(qrecv.at[i // 2, i % 2], q_sem.at[i])
    arrived(cbuf, c_sem)

    tails = qrecv[0, 0, 32:QPAD, :128].astype(F32) + qrecv[1, 0, 32:QPAD, :128].astype(F32)
    flat = tails[8:9] + tails[9:10]
    total = jnp.sum(jnp.where(diagonal, flat, 0.0), axis=1, keepdims=True)
    factor = lax.rsqrt(total * (1.0 / FULL) + EPS)
    cosine = cos_ref[...]
    sine = sin_ref[...]

    def rope(u):
        return u * cosine + pltpu.roll(u, HEAD // 2, 1) * sine

    heads = []
    news = []
    for p in (0, 1):
        both = qrecv[0, p].astype(F32) + qrecv[1, p].astype(F32)
        both = both[:QROWS] * factor
        for i in range(4):
            heads.append(rope(both[:, i * HEAD : (i + 1) * HEAD]))
        news.append(both[:, 512:640])
    query = jnp.concatenate(heads, axis=0).astype(BF)
    no_rows = jnp.zeros((128 - QROWS, HEAD), F32)
    key_new = rope(news[0].astype(BF).astype(F32))
    key_new = jnp.concatenate([key_new, no_rows], axis=0).astype(BF)
    value_new = jnp.concatenate([news[1], no_rows], axis=0).astype(BF)
    keys = cbuf[:, :, :, :HEAD].reshape(640, HEAD)
    values = cbuf[:, :, :, HEAD:].reshape(640, HEAD)

    contract_last = (((1,), (1,)), ((), ()))
    inv_root = 1.0 / math.sqrt(HEAD)
    scores_old = lax.dot_general(query, keys, contract_last, preferred_element_type=F32) * inv_root
    scores_new = (
        lax.dot_general(query, key_new, contract_last, preferred_element_type=F32) * inv_root
    )
    scores_old = jnp.where(old_bias == 0.0, scores_old, -1e30)
    scores_new = jnp.where(new_bias == 0.0, scores_new, -1e30)
    top = jnp.maximum(
        jnp.max(scores_old, axis=1, keepdims=True), jnp.max(scores_new, axis=1, keepdims=True)
    )
    exp_old = jnp.exp(scores_old - top)
    exp_new = jnp.exp(scores_new - top)
    totals = jnp.sum(exp_old, axis=1, keepdims=True) + jnp.sum(exp_new, axis=1, keepdims=True)
    probs_old = (exp_old / totals).astype(BF)
    probs_new = (exp_new / totals).astype(BF)
    attended = jnp.dot(probs_old, values, preferred_element_type=F32)
    attended = attended + jnp.dot(probs_new, value_new, preferred_element_type=F32)
    for p in (0, 1):
        side = jnp.concatenate(
            [attended[(4 * p + i) * QROWS : (4 * p + i + 1) * QROWS] for i in range(4)], axis=1
        )
        asend[p] = jnp.concatenate([side, jnp.zeros((QPAD - QROWS, 512), F32)], axis=0).astype(BF)
        for y_ in (0, 1):
            to(asend.at[p], arecv.at[b], a_sem.at[b], dpi(x, y_, c), z * NB + p * 2 + yh)

    wout.last(bset)
    wout.last(1 - bset)
    wout.finish()
    for i in range(NB):
        arrived(arecv.at[i], a_sem.at[i])
    att[...] = jnp.concatenate(
        [arecv[i].astype(F32)[:QROWS] for i in range(NB)], axis=0
    ).astype(BF)

    cross = ((2, 0), (3, 1), (0, 2), (1, 3))
    if_match = [(4, i) for i in range(4)]
    if_match += [item for i, j in cross for item in ((2, i), (6, j))]
    if_match += [(0, i) for i in (2, 0, 3, 1)]
    if_not = [item for i, j in cross for item in ((3, i), (5, j))]
    if_not += [item for i, j in cross for item in ((1, i), (7, j))]
    for n in range(16):
        (d_m, i_m), (d_n, i_n) = if_match[n], if_not[n]
        delta = jnp.where(match, d_m, d_n)
        b_ = jnp.where(match, i_m, i_n)
        k = ((z + delta) % NZ) // 2
        reach = jnp.where(b_ < 2, 4, 3)
        is_end = delta == 0
        c_ = b_ // 2
        h = b_ % 2
        part = jnp.dot(
            att[:, :256], wobuf[0, k, c_, :, pl.ds(h * 256, 256)], preferred_element_type=F32
        )
        acc[...] = part + jnp.dot(
            att[:, 256:], wobuf[1, k, c_, :, pl.ds(h * 256, 256)], preferred_element_type=F32
        )
        from_left = delta + 1 <= reach
        from_right = jnp.logical_or(delta > reach + 1, is_end)
        index = k * NB + b_

        @pl.when(from_left)
        def _(index=index, k=k, b_=b_):
            arrived(rright.at[k, b_], rr_sem.at[index])
            acc[...] += rright[k, b_].astype(F32)

        @pl.when(from_right)
        def _(index=index, k=k, b_=b_):
            arrived(rleft.at[k, b_], rl_sem.at[index])
            acc[...] += rleft[k, b_].astype(F32)

        if n >= 12:

            @pl.when(jnp.logical_and(is_end, pair == 0))
            def _(k=k, b_=b_):
                acc[...] += xb[k, b_, :NROWS].astype(F32)

        src = sbuf.at[k, b_]
        src[...] = acc[...].astype(BF)
        remote(
            src,
            rright.at[k, b_],
            rr_sem.at[index],
            right_z,
            jnp.logical_and(delta >= 1, delta <= reach),
        )
        remote(src, rleft.at[k, b_], rl_sem.at[index], left_z, delta > reach)
        if n >= 12:
            dp_ = dpi(x, bset, c)
            tn_ = z * NB + b_
            here = jnp.logical_and(dp_ == dp, tn_ == tn)
            remote(
                src,
                frecv.at[pair],
                f_sem.at[pair],
                dev(dp_, tn_),
                jnp.logical_and(is_end, jnp.logical_not(here)),
            )
            local(src, frecv.at[pair], f_sem.at[pair], jnp.logical_and(is_end, here))

    for p in (0, 1):
        arrived(frecv.at[p], f_sem.at[p])
    hidden = frecv[0].astype(F32) + frecv[1].astype(F32)
    hidden = jnp.concatenate([hidden, jnp.zeros((256 - NROWS, 256), F32)], axis=0).astype(BF)
    to_row = lax.broadcasted_iota(jnp.int32, (NROWS, 256), 0)
    from_row = lax.broadcasted_iota(jnp.int32, (NROWS, 256), 1)
    order = jnp.where(from_row == (to_row % 40) * 4 + to_row // 40, 1.0, 0.0).astype(BF)
    out_ref[...] = jnp.dot(order, hidden, preferred_element_type=F32).astype(BF)

    for cond, copy in pending:
        if cond is None:
            copy.wait_send()
        else:
            pl.when(cond)(copy.wait_send)

    def lookup_sent(e, carry):
        dp2, copy = lookup_copy(e)
        pl.when(dp2 != dp)(copy.wait_send)
        return carry

    lax.fori_loop(0, 8, lookup_sent, 0)


def body(
    token_ids, lengths, embed_table, norm_gain, w_query, key_value_weight, w_out, key_value_cache
):
    table = embed_table.reshape(16, -1)
    frequency = THETA ** (-(np.arange(64) / 64))
    frequency = jnp.asarray(np.concatenate([frequency, frequency])[None], F32)
    keyval = key_value_weight.T
    cache = key_value_cache.reshape(40, 16, 256)

    vmem = pl.BlockSpec(memory_space=pltpu.VMEM)
    anywhere = pl.BlockSpec(memory_space=pl.ANY)
    dma = pltpu.SemaphoreType.DMA
    out = pl.pallas_call(
        kernel,
        out_shape=jax.ShapeDtypeStruct((NROWS, 256), BF),
        in_specs=[vmem, vmem, anywhere, vmem, vmem, anywhere, anywhere, anywhere, anywhere],
        out_specs=vmem,
        scratch_shapes=[
            pltpu.VMEM((16, 81920), BF),
            pltpu.VMEM((16, 4, 40), jnp.int32),
            pltpu.SMEM((16, 4, 40), jnp.int32),
            pltpu.VMEM((8, 2, 16, 256), BF),
            pltpu.VMEM((QROWS, HEAD), F32),
            pltpu.VMEM((QROWS, HEAD), F32),
            pltpu.VMEM((16, 2, 16, 256), BF),
            pltpu.VMEM((2, XROWS, 256), BF),
            pltpu.VMEM((4, NB, XROWS, 256), BF),
            pltpu.VMEM((2, NX, 2, 640, 256), BF),
            pltpu.VMEM((2, NX, 2, 256, 512), BF),
            pltpu.VMEM((NB, 10, 16, 256), BF),
            pltpu.VMEM((NB, QPAD, 640), BF),
            pltpu.VMEM((2, 2, QPAD, 640), BF),
            pltpu.VMEM((2, QPAD, 512), BF),
            pltpu.VMEM((NB, QPAD, 512), BF),
            pltpu.VMEM((NROWS, 512), BF),
            pltpu.VMEM((NROWS, 512), F32),
            pltpu.VMEM((NROWS, 128), F32),
            pltpu.VMEM((NROWS, 128), F32),
            pltpu.VMEM((NROWS, 256), F32),
            pltpu.VMEM((4, NB, NROWS, 256), BF),
            pltpu.VMEM((4, NB, NROWS, 256), BF),
            pltpu.VMEM((4, NB, NROWS, 256), BF),
            pltpu.VMEM((2, NROWS, 256), BF),
            dma((192,)),
            dma((3,)),
            dma((16,)),
            dma,
            dma((16,)),
            dma((32,)),
            dma((32,)),
            dma,
            dma((4,)),
            dma((4,)),
            dma((16,)),
            dma((16,)),
            dma((2,)),
        ],
        compiler_params=pltpu.CompilerParams(
            collective_id=0, has_side_effects=True, vmem_limit_bytes=56 * 1024 * 1024
        ),
        name="decode_block",
    )(token_ids, lengths[None], table, norm_gain, frequency, w_query, keyval, w_out, cache)
    return out.reshape(4, 40, 256)


def solution(mesh):
    in_specs = (
        P(None, "dp"),
        P("dp"),
        P(None, "tensor", "dp", None),
        P("tensor"),
        P("dp", "tensor"),
        P("dp", "tensor"),
        P("tensor", "dp"),
        P("dp", "tensor", None, None),
    )
    out_specs = P(None, "dp", "tensor")
    return jax.shard_map(body, mesh=mesh, in_specs=in_specs, out_specs=out_specs, check_vma=False)
```

```python
import functools
import math

import jax
import jax.numpy as jnp
import numpy as np
from jax import lax
from jax.experimental import pallas as pl
from jax.experimental.pallas import tpu as pltpu
from jax.sharding import PartitionSpec as P

EPS = 1e-06
THETA = 1000000.0
BF = jnp.bfloat16
F32 = jnp.float32

NX = 4
NZ = 8
NB = 4
QROWS = 40
QPAD = 48
NROWS = 160
XROWS = 176
HEAD = 128
FULL = 8192

MESH = pl.DeviceIdType.MESH


def kernel(
    tok_ref,
    len_ref,
    table_ref,
    gain_ref,
    freq_ref,
    wq_ref,
    wkv_ref,
    wo_ref,
    cache_ref,
    out_ref,
    tab,
    tokv,
    toks,
    lsend,
    cos_ref,
    sin_ref,
    lrecv,
    xt,
    xb,
    wbuf,
    wobuf,
    cbuf,
    qsend,
    qrecv,
    asend,
    arecv,
    att,
    qacc,
    kvacc,
    ssq,
    acc,
    sbuf,
    rright,
    rleft,
    frecv,
    send_sem,
    loc_sem,
    tok_sem,
    l_sem,
    x_sem,
    w_sem,
    wo_sem,
    c_sem,
    q_sem,
    a_sem,
    rr_sem,
    rl_sem,
    f_sem,
):
    dp = lax.axis_index("dp")
    tn = lax.axis_index("tensor")
    x = dp // 4
    yh = (dp // 2) % 2
    c = dp % 2
    z = tn // 4
    b = tn % 4
    zpar = z % 2
    match = zpar == yh
    pair = b // 2
    bset = b % 2

    def dev(dp_, tn_):
        return {"dp": dp_, "tensor": tn_}

    def dpi(x_, yh_, c_):
        return (x_ * 2 + yh_) * 2 + c_

    pending = []
    pending_out = []
    counter = [0]

    def remote(src, dst, rsem, where, cond=None, sink=pending):
        n = counter[0]
        counter[0] += 1
        copy = pltpu.make_async_remote_copy(
            src_ref=src,
            dst_ref=dst,
            send_sem=send_sem.at[n],
            recv_sem=rsem,
            device_id=where,
            device_id_type=MESH,
        )
        if cond is None:
            copy.start()
        else:
            pl.when(cond)(copy.start)
        sink.append((cond, copy))

    def sent(sink, count=None):
        done = sink[:count]
        del sink[:count]
        for cond, copy in done:
            if cond is None:
                copy.wait_send()
            else:
                pl.when(cond)(copy.wait_send)

    def local(src, dst, sem, cond=None):
        copy = pltpu.make_async_copy(src, dst, sem)
        if cond is None:
            copy.start()
        else:
            pl.when(cond)(copy.start)

    def arrived(dst, sem):
        pltpu.make_async_copy(dst, dst, sem).wait()

    def to(src, dst, rsem, dp_, tn_):
        here = jnp.logical_and(dp_ == dp, tn_ == tn)
        remote(src, dst, rsem, dev(dp_, tn_), jnp.logical_not(here))
        local(src, dst, rsem, here)

    xr = (x + 1) % NX
    xl = (x + NX - 1) % NX
    xo = (x + 2) % NX
    zr = (z + 1) % NZ
    zl = (z + NZ - 1) % NZ
    right_z = dev(dp, zr * NB + b)
    left_z = dev(dp, zl * NB + b)

    table_copy = pltpu.make_async_copy(table_ref, tab, loc_sem.at[0])
    table_copy.start()
    local(tok_ref, tokv.at[dp], tok_sem.at[dp])
    own_shard = wbuf.at[bset, x, c]
    own_sem = w_sem.at[((bset * NX + x) * 2 + c) * 2]
    local(wq_ref, own_shard.at[pl.ds(0, 512)], own_sem)
    for h in (0, 1):
        local(
            wkv_ref.at[:, pl.ds(h * 256, 256)], own_shard.at[pl.ds(512 + h * 64, 64)], own_sem
        )

    barrier = pltpu.get_barrier_semaphore()
    partners = 0
    for i in range(1, 16):
        pl.semaphore_signal(barrier, inc=1, device_id=dev((dp + i) % 16, tn), device_id_type=MESH)
        partners += 1
    for i in range(1, 8):
        if i == 4:
            continue
        u = (yh * 4 + b + i) % 8
        pl.semaphore_signal(
            barrier, inc=1, device_id=dev(dpi(x, u // 4, c), z * NB + u % 4), device_id_type=MESH
        )
        partners += 1
    for where in (right_z, left_z):
        pl.semaphore_signal(barrier, inc=1, device_id=where, device_id_type=MESH)
        partners += 1

    pl.semaphore_wait(barrier, partners)

    for i in range(1, 16):
        e_ = (x * 2 + c + 8 - i % 8) % 8
        there = dpi(e_ // 2, (yh + i // 8) % 2, e_ % 2)
        remote(tok_ref, tokv.at[dp], tok_sem.at[dp], dev(there, tn))

    class Gather:
        def __init__(self, buf, sem, half, sink):
            self.buf, self.sem, self.half, self.sink = buf, sem, half, sink

        def slot(self, q, x_, c_, h=None):
            ref = self.buf.at[q, x_, c_]
            if h is None:
                return ref
            return ref.at[pl.ds(h * self.half, self.half)]

        def s(self, q, x_, c_, h=0):
            return self.sem.at[((q * NX + x_) * 2 + c_) * 2 + h]

        def send(self, src, q, x_, where):
            remote(src, self.slot(q, x_, c), self.s(q, x_, c), where, sink=self.sink)

        def to_pair(self):
            own = (bset, x)
            src = self.slot(*own, c)
            arrived(src, self.s(*own, c))
            self.send(src, *own, dev(dp, z * NB + pair * 2 + 1 - bset))

        def first(self):
            own = (bset, x)
            src = self.slot(*own, c)
            self.send(src, *own, dev(dpi(xr, yh, c), tn))
            self.send(src, *own, dev(dpi(xl, yh, c), tn))
            self.send(src, *own, dev(dpi(x, yh, 1 - c), tn))

        def second(self):
            q = 1 - bset
            arrived(self.slot(q, x, c), self.s(q, x, c))
            src = self.slot(q, x, c)
            self.send(src, q, x, dev(dpi(xr, yh, c), tn))
            self.send(src, q, x, dev(dpi(xl, yh, c), tn))
            self.send(src, q, x, dev(dpi(x, yh, 1 - c), tn))

        def relay(self, q):
            for x_, h, to_x in ((xl, 0, xr), (xr, 1, xl)):
                arrived(self.slot(q, x_, c), self.s(q, x_, c))
                remote(
                    self.slot(q, x_, c, h),
                    self.slot(q, x_, c, h),
                    self.s(q, x_, c, h),
                    dev(dpi(to_x, yh, c), tn),
                    sink=self.sink,
                )
                self.send(self.slot(q, x_, c), q, x_, dev(dpi(x, yh, 1 - c), tn))

        def last(self, q):
            for h in (0, 1):
                arrived(self.slot(q, xo, c, h), self.s(q, xo, c, h))
            self.send(self.slot(q, xo, c), q, xo, dev(dpi(x, yh, 1 - c), tn))

        def finish(self):
            for q in (0, 1):
                for x_ in range(NX):
                    arrived(self.slot(q, x_, 1 - c), self.s(q, x_, 1 - c))

    wqkv = Gather(wbuf, w_sem, 320, pending)
    wout = Gather(wobuf, wo_sem, 128, pending_out)
    wqkv.to_pair()
    wqkv.first()
    local(wo_ref, wout.slot(bset, x, c), wout.s(bset, x, c))

    place = x * 2 + c

    def source(i):
        e = (place + i % 8) % 8
        s = (yh + i // 8) % 2
        return e, s, dpi(e // 2, s, e % 2)

    def to_scalar(i):
        _, _, d2 = source(i)
        return pltpu.make_async_copy(tokv.at[d2], toks.at[d2], loc_sem.at[1 + i % 2])

    def fetch(i):
        _, _, d2 = source(i)
        arrived(tokv.at[d2], tok_sem.at[d2])
        to_scalar(i).start()

    fetch(0)
    table_copy.wait()

    lane = lax.broadcasted_iota(jnp.int32, (16, 128), 1)
    wide = lax.broadcasted_iota(jnp.int32, (16, 256), 1)
    feature = lax.broadcasted_iota(jnp.int32, (16, 256), 0)
    gain_column = jnp.sum(
        jnp.where(wide == dp * 16 + feature, gain_ref[...].astype(F32)[None], 0.0),
        axis=1,
        keepdims=True,
    )
    gain_tail = jnp.where(lane == NROWS - 128, gain_column, 0.0)
    lookup_base = counter[0]
    counter[0] += 8

    def lookup_copy(e):
        dp2 = dpi(e // 2, zpar, e % 2)
        return dp2, pltpu.make_async_remote_copy(
            src_ref=lsend.at[e],
            dst_ref=lrecv.at[dp],
            send_sem=send_sem.at[lookup_base + e],
            recv_sem=l_sem,
            device_id=dev(dp2, tn),
            device_id_type=MESH,
        )

    def lookup(i, carry):
        e, s, d2 = source(i)
        pl.when(i < 15)(lambda: fetch(i + 1))
        to_scalar(i).wait()
        for half, count in ((0, 128), (1, NROWS - 128)):
            found = jnp.zeros((16, 128), F32) if half == 0 else gain_tail
            for n in range(count):
                row = half * 128 + n
                token = toks[d2, row % 4, row // 4]
                block = lax.shift_right_logical(token, 7)
                tile = tab[:, pl.ds(block * 128, 128)].astype(F32)
                picked = jnp.where(lane == jnp.bitwise_and(token, 127), tile, 0.0)
                found = jnp.where(lane == n, jnp.sum(picked, axis=1, keepdims=True), found)
            lsend[e, s, :, pl.ds(half * 128, 128)] = found.astype(BF)

        @pl.when(i >= 8)
        def _():
            dp2, copy = lookup_copy(e)
            pl.when(dp2 != dp)(copy.start)
            pl.when(dp2 == dp)(pltpu.make_async_copy(lsend.at[e], lrecv.at[dp], l_sem).start)

        return carry

    lax.fori_loop(0, 16, lookup, 0)
    wqkv.second()
    wqkv.relay(bset)

    k_here = z // 2

    pl.when(match)(lambda: arrived(lrecv, l_sem))
    for s in (0, 1):

        @pl.when(match)
        def _(s=s):
            features = lrecv[:, s].reshape(256, 256).astype(F32)
            xt[s] = features.T[:XROWS].astype(BF)

        for h in (0, 1):
            b2 = (1 - pair if h == 0 else pair) * 2 + s
            here = b2 == b
            dst = xb.at[k_here, b]
            sem = x_sem.at[k_here * NB + b]
            remote(
                xt.at[s],
                dst,
                sem,
                dev(dp, z * NB + b2),
                jnp.logical_and(match, jnp.logical_not(here)),
            )
            local(xt.at[s], dst, sem, jnp.logical_and(match, here))

    def by_b(values):
        return jnp.where(
            b == 0, values[0], jnp.where(b == 1, values[1], jnp.where(b == 2, values[2], values[3]))
        )

    nearest = [by_b(v) for v in ((0, 1, 2, 3), (1, 0, 3, 2), (2, 2, 1, 1), (3, 3, 0, 0))]
    if_match = [(0, i) for i in range(4)]
    if_match += [(d, i) for i in range(4) for d in (2, 6)]
    if_match += [(4, i) for i in range(4)]
    if_not = [(d, i) for i in range(4) for d in (1, 7)]
    if_not += [(d, i) for i in range(4) for d in (3, 5)]
    blocks = []
    for (d_m, i_m), (d_n, i_n) in zip(if_match, if_not):
        delta = jnp.where(match, d_m, d_n)
        b_ = jnp.where(match, nearest[i_m], nearest[i_n])
        blocks.append((delta, ((z - delta + NZ) % NZ) // 2, b_))

    row40 = lax.broadcasted_iota(jnp.int32, (QROWS, 128), 0)
    lane40 = lax.broadcasted_iota(jnp.int32, (QROWS, 128), 1)

    def angles():
        lengths = len_ref[...].astype(F32)
        row_of = lax.broadcasted_iota(jnp.int32, (QROWS, 40), 0) // 4 + b * 10
        all_rows = lax.broadcasted_iota(jnp.int32, (QROWS, 40), 1)
        length = jnp.sum(jnp.where(all_rows == row_of, lengths, 0.0), axis=1, keepdims=True)
        turn = (length + (row40 % 4).astype(F32)) * freq_ref[...]
        cos_ref[...] = jnp.cos(turn)
        sin_ref[...] = jnp.where(lane40 < HEAD // 2, -1.0, 1.0) * jnp.sin(turn)
        return length

    def forward(n):
        delta, k, b_ = blocks[n]
        reach = jnp.where(b_ < 2, 4, 3)
        block = xb.at[k, b_]
        sem = x_sem.at[k * NB + b_]
        arrived(block, sem)
        if n < 4:
            onward = delta == 0
        else:
            onward = False
        onward = jnp.logical_or(
            onward, jnp.logical_and(delta > reach, 8 - delta < 7 - reach)
        )
        remote(block, block, sem, right_z, delta < reach)
        remote(block, block, sem, left_z, onward)

    def project(n):
        _, k, b_ = blocks[n]
        c_ = b_ // 2
        h = b_ % 2
        raw = xb[k, b_].astype(F32)
        rows = raw[:NROWS]
        gain = raw[NROWS : NROWS + 1]
        scaled = (rows * gain).astype(BF)
        square = rows * rows
        square = square[:, :128] + square[:, 128:]
        parts = [
            jnp.dot(scaled, wbuf[q, k, c_, pl.ds(h * 256, 256)], preferred_element_type=F32)
            for q in (0, 1)
        ]
        keyval = jnp.concatenate(
            [wbuf[q, k, c_, pl.ds(512 + h * 64, 64)] for q in (0, 1)], axis=0
        )
        kv = lax.dot_general(
            scaled, keyval, (((1,), (1,)), ((), ())), preferred_element_type=F32
        )
        if n == 0:
            ssq[...] = square
            qacc[:, :256] = parts[0]
            qacc[:, 256:] = parts[1]
            kvacc[...] = kv
        else:
            ssq[...] += square
            qacc[:, :256] += parts[0]
            qacc[:, 256:] += parts[1]
            kvacc[...] += kv

    forward(0)
    wqkv.relay(1 - bset)
    forward(1)
    wqkv.last(bset)
    forward(2)
    forward(3)
    wout.to_pair()
    wqkv.last(1 - bset)
    for n in range(4, 16):
        forward(n)
        if n == 5:
            wout.first()
        if n == 8:
            for i in range(NB):
                b2 = (b + i) % NB
                to(cache_ref.at[pl.ds(b2 * 10, 10)], cbuf.at[b], c_sem, dp, z * NB + b2)
        if n == 9:
            wout.second()
        if n == 11:
            wqkv.finish()
            for m in range(11):
                project(m)
        if n >= 11:
            project(n)
        if n == 14:
            wout.relay(bset)

    before_q = len(pending)

    diagonal = row40 == lane40
    row8 = lax.broadcasted_iota(jnp.int32, (8, 128), 0)
    for i in range(NB):
        total = jnp.sum(ssq[i * QROWS : (i + 1) * QROWS], axis=1, keepdims=True)
        flat = jnp.sum(jnp.where(diagonal, total, 0.0), axis=0, keepdims=True)
        high = flat.astype(BF).astype(F32)
        low = flat - high
        tail = jnp.where(row8 == 0, high, jnp.where(row8 == 1, low, 0.0))
        tail = jnp.concatenate([tail, jnp.zeros((8, 512), F32)], axis=1)
        body_rows = jnp.concatenate(
            [qacc[i * QROWS : (i + 1) * QROWS], kvacc[i * QROWS : (i + 1) * QROWS]], axis=1
        )
        qsend[i] = jnp.concatenate([body_rows, tail], axis=0).astype(BF)
        to(
            qsend.at[i],
            qrecv.at[yh, pair],
            q_sem.at[yh * 2 + pair],
            dpi(x, bset, c),
            z * NB + i,
        )

    wout.relay(1 - bset)

    length = angles()
    col = lax.broadcasted_iota(jnp.int32, (QROWS, 640), 1)
    row = lax.broadcasted_iota(jnp.int32, (QROWS, 640), 0) // 4
    within = col % 160
    position = (col // 160) * 16 + within % 16
    old_ok = jnp.logical_and(within // 16 == row, position.astype(F32) < length)
    new_ok = jnp.logical_and(
        lane40 // 4 == row40 // 4, jnp.logical_and(lane40 <= row40, lane40 < QROWS)
    )
    old_bias = jnp.where(old_ok, 0.0, -1e30)
    new_bias = jnp.where(new_ok, 0.0, -1e30)
    old_bias = jnp.concatenate([old_bias] * 8, axis=0)
    new_bias = jnp.concatenate([new_bias] * 8, axis=0)
    sent(pending, before_q)

    def lookup_sent(e, carry):
        dp2, copy = lookup_copy(e)
        pl.when(dp2 != dp)(copy.wait_send)
        return carry

    lax.fori_loop(0, 8, lookup_sent, 0)

    for i in range(NB):
        arrived(qrecv.at[i // 2, i % 2], q_sem.at[i])
    arrived(cbuf, c_sem)

    tails = qrecv[0, 0, 32:QPAD, :128].astype(F32) + qrecv[1, 0, 32:QPAD, :128].astype(F32)
    flat = tails[8:9] + tails[9:10]
    total = jnp.sum(jnp.where(diagonal, flat, 0.0), axis=1, keepdims=True)
    factor = lax.rsqrt(total * (1.0 / FULL) + EPS)
    cosine = cos_ref[...]
    sine = sin_ref[...]

    def rope(u):
        return u * cosine + pltpu.roll(u, HEAD // 2, 1) * sine

    heads = []
    news = []
    for p in (0, 1):
        both = qrecv[0, p].astype(F32) + qrecv[1, p].astype(F32)
        both = both[:QROWS] * factor
        for i in range(4):
            heads.append(rope(both[:, i * HEAD : (i + 1) * HEAD]))
        news.append(both[:, 512:640])
    query = jnp.concatenate(heads, axis=0).astype(BF)
    no_rows = jnp.zeros((128 - QROWS, HEAD), F32)
    key_new = rope(news[0].astype(BF).astype(F32))
    key_new = jnp.concatenate([key_new, no_rows], axis=0).astype(BF)
    value_new = jnp.concatenate([news[1], no_rows], axis=0).astype(BF)
    keys = cbuf[:, :, :, :HEAD].reshape(640, HEAD)
    values = cbuf[:, :, :, HEAD:].reshape(640, HEAD)

    contract_last = (((1,), (1,)), ((), ()))
    inv_root = 1.0 / math.sqrt(HEAD)
    scores_old = lax.dot_general(query, keys, contract_last, preferred_element_type=F32) * inv_root
    scores_new = (
        lax.dot_general(query, key_new, contract_last, preferred_element_type=F32) * inv_root
    )
    scores_old = jnp.where(old_bias == 0.0, scores_old, -1e30)
    scores_new = jnp.where(new_bias == 0.0, scores_new, -1e30)
    top = jnp.maximum(
        jnp.max(scores_old, axis=1, keepdims=True), jnp.max(scores_new, axis=1, keepdims=True)
    )
    exp_old = jnp.exp(scores_old - top)
    exp_new = jnp.exp(scores_new - top)
    totals = jnp.sum(exp_old, axis=1, keepdims=True) + jnp.sum(exp_new, axis=1, keepdims=True)
    share = 1.0 / totals
    probs_old = (exp_old * share).astype(BF)
    probs_new = (exp_new * share).astype(BF)
    attended = jnp.dot(probs_old, values, preferred_element_type=F32)
    attended = attended + jnp.dot(probs_new, value_new, preferred_element_type=F32)
    for p in (0, 1):
        side = jnp.concatenate(
            [attended[(4 * p + i) * QROWS : (4 * p + i + 1) * QROWS] for i in range(4)], axis=1
        )
        asend[p] = jnp.concatenate([side, jnp.zeros((QPAD - QROWS, 512), F32)], axis=0).astype(BF)
        for y_ in (0, 1):
            to(asend.at[p], arecv.at[b], a_sem.at[b], dpi(x, y_, c), z * NB + p * 2 + yh)

    wout.last(bset)
    wout.last(1 - bset)
    wout.finish()
    sent(pending_out)
    for i in range(NB):
        arrived(arecv.at[i], a_sem.at[i])
    att[...] = jnp.concatenate(
        [arecv[i].astype(F32)[:QROWS] for i in range(NB)], axis=0
    ).astype(BF)

    cross = ((2, 0), (3, 1), (0, 2), (1, 3))
    if_match = [(4, i) for i in range(4)]
    if_match += [item for i, j in cross for item in ((2, i), (6, j))]
    if_match += [(0, i) for i in (2, 0, 3, 1)]
    if_not = [item for i, j in cross for item in ((3, i), (5, j))]
    if_not += [item for i, j in cross for item in ((1, i), (7, j))]
    for n in range(16):
        (d_m, i_m), (d_n, i_n) = if_match[n], if_not[n]
        delta = jnp.where(match, d_m, d_n)
        b_ = jnp.where(match, i_m, i_n)
        k = ((z + delta) % NZ) // 2
        reach = jnp.where(b_ < 2, 4, 3)
        is_end = delta == 0
        c_ = b_ // 2
        h = b_ % 2
        part = jnp.dot(
            att[:, :256], wobuf[0, k, c_, :, pl.ds(h * 256, 256)], preferred_element_type=F32
        )
        acc[...] = part + jnp.dot(
            att[:, 256:], wobuf[1, k, c_, :, pl.ds(h * 256, 256)], preferred_element_type=F32
        )
        from_left = delta + 1 <= reach
        from_right = jnp.logical_or(delta > reach + 1, is_end)
        index = k * NB + b_

        @pl.when(from_left)
        def _(index=index, k=k, b_=b_):
            arrived(rright.at[k, b_], rr_sem.at[index])
            acc[...] += rright[k, b_].astype(F32)

        @pl.when(from_right)
        def _(index=index, k=k, b_=b_):
            arrived(rleft.at[k, b_], rl_sem.at[index])
            acc[...] += rleft[k, b_].astype(F32)

        if n == 12:
            before_end = len(pending)
        if n >= 12:

            @pl.when(jnp.logical_and(is_end, pair == 0))
            def _(k=k, b_=b_):
                acc[...] += xb[k, b_, :NROWS].astype(F32)

        src = sbuf.at[k, b_]
        src[...] = acc[...].astype(BF)
        remote(
            src,
            rright.at[k, b_],
            rr_sem.at[index],
            right_z,
            jnp.logical_and(delta >= 1, delta <= reach),
        )
        remote(src, rleft.at[k, b_], rl_sem.at[index], left_z, delta > reach)
        if n >= 12:
            dp_ = dpi(x, bset, c)
            tn_ = z * NB + b_
            here = jnp.logical_and(dp_ == dp, tn_ == tn)
            remote(
                src,
                frecv.at[pair],
                f_sem.at[pair],
                dev(dp_, tn_),
                jnp.logical_and(is_end, jnp.logical_not(here)),
            )
            local(src, frecv.at[pair], f_sem.at[pair], jnp.logical_and(is_end, here))

    sent(pending, before_end)
    for p in (0, 1):
        arrived(frecv.at[p], f_sem.at[p])
    hidden = frecv[0].astype(F32) + frecv[1].astype(F32)
    hidden = jnp.concatenate([hidden, jnp.zeros((256 - NROWS, 256), F32)], axis=0).astype(BF)
    to_row = lax.broadcasted_iota(jnp.int32, (NROWS, 256), 0)
    from_row = lax.broadcasted_iota(jnp.int32, (NROWS, 256), 1)
    order = jnp.where(from_row == (to_row % 40) * 4 + to_row // 40, 1.0, 0.0).astype(BF)
    out_ref[...] = jnp.dot(order, hidden, preferred_element_type=F32).astype(BF)

    sent(pending)


def body(
    token_ids, lengths, embed_table, norm_gain, w_query, key_value_weight, w_out, key_value_cache
):
    table = embed_table.reshape(16, -1)
    frequency = THETA ** (-(np.arange(64) / 64))
    frequency = jnp.asarray(np.concatenate([frequency, frequency])[None], F32)
    keyval = key_value_weight.T
    cache = key_value_cache.reshape(40, 16, 256)

    vmem = pl.BlockSpec(memory_space=pltpu.VMEM)
    anywhere = pl.BlockSpec(memory_space=pl.ANY)
    dma = pltpu.SemaphoreType.DMA
    out = pl.pallas_call(
        kernel,
        out_shape=jax.ShapeDtypeStruct((NROWS, 256), BF),
        in_specs=[vmem, vmem, anywhere, vmem, vmem, anywhere, anywhere, anywhere, anywhere],
        out_specs=vmem,
        scratch_shapes=[
            pltpu.VMEM((16, 81920), BF),
            pltpu.VMEM((16, 4, 40), jnp.int32),
            pltpu.SMEM((16, 4, 40), jnp.int32),
            pltpu.VMEM((8, 2, 16, 256), BF),
            pltpu.VMEM((QROWS, HEAD), F32),
            pltpu.VMEM((QROWS, HEAD), F32),
            pltpu.VMEM((16, 2, 16, 256), BF),
            pltpu.VMEM((2, XROWS, 256), BF),
            pltpu.VMEM((4, NB, XROWS, 256), BF),
            pltpu.VMEM((2, NX, 2, 640, 256), BF),
            pltpu.VMEM((2, NX, 2, 256, 512), BF),
            pltpu.VMEM((NB, 10, 16, 256), BF),
            pltpu.VMEM((NB, QPAD, 640), BF),
            pltpu.VMEM((2, 2, QPAD, 640), BF),
            pltpu.VMEM((2, QPAD, 512), BF),
            pltpu.VMEM((NB, QPAD, 512), BF),
            pltpu.VMEM((NROWS, 512), BF),
            pltpu.VMEM((NROWS, 512), F32),
            pltpu.VMEM((NROWS, 128), F32),
            pltpu.VMEM((NROWS, 128), F32),
            pltpu.VMEM((NROWS, 256), F32),
            pltpu.VMEM((4, NB, NROWS, 256), BF),
            pltpu.VMEM((4, NB, NROWS, 256), BF),
            pltpu.VMEM((4, NB, NROWS, 256), BF),
            pltpu.VMEM((2, NROWS, 256), BF),
            dma((192,)),
            dma((3,)),
            dma((16,)),
            dma,
            dma((16,)),
            dma((32,)),
            dma((32,)),
            dma,
            dma((4,)),
            dma((4,)),
            dma((16,)),
            dma((16,)),
            dma((2,)),
        ],
        compiler_params=pltpu.CompilerParams(
            collective_id=0, has_side_effects=True, vmem_limit_bytes=56 * 1024 * 1024
        ),
        name="decode_block",
    )(token_ids, lengths[None], table, norm_gain, frequency, w_query, keyval, w_out, cache)
    return out.reshape(4, 40, 256)


def solution(mesh):
    in_specs = (
        P(None, "dp"),
        P("dp"),
        P(None, "tensor", "dp", None),
        P("tensor"),
        P("dp", "tensor"),
        P("dp", "tensor"),
        P("tensor", "dp"),
        P("dp", "tensor", None, None),
    )
    out_specs = P(None, "dp", "tensor")
    return jax.shard_map(body, mesh=mesh, in_specs=in_specs, out_specs=out_specs, check_vma=False)
```

```python
import functools
import math

import jax
import jax.numpy as jnp
import numpy as np
from jax import lax
from jax.experimental import pallas as pl
from jax.experimental.pallas import tpu as pltpu
from jax.sharding import PartitionSpec as P

EPS = 1e-06
THETA = 1000000.0
BF = jnp.bfloat16
F32 = jnp.float32

NX = 4
NZ = 8
NB = 4
QROWS = 40
QPAD = 48
NROWS = 160
XROWS = 176
HEAD = 128
FULL = 8192

MESH = pl.DeviceIdType.MESH


def kernel(
    tok_ref,
    len_ref,
    table_ref,
    gain_ref,
    freq_ref,
    wq_ref,
    wkv_ref,
    wo_ref,
    cache_ref,
    out_ref,
    tab,
    tokv,
    toks,
    lsend,
    cos_ref,
    sin_ref,
    lrecv,
    xt,
    xb,
    wbuf,
    wobuf,
    cbuf,
    qsend,
    qrecv,
    asend,
    arecv,
    att,
    qacc,
    kvacc,
    ssq,
    acc,
    sbuf,
    rright,
    rleft,
    frecv,
    send_sem,
    loc_sem,
    tok_sem,
    l_sem,
    x_sem,
    w_sem,
    wo_sem,
    c_sem,
    q_sem,
    a_sem,
    rr_sem,
    rl_sem,
    f_sem,
):
    dp = lax.axis_index("dp")
    tn = lax.axis_index("tensor")
    x = dp // 4
    yh = (dp // 2) % 2
    c = dp % 2
    z = tn // 4
    b = tn % 4
    zpar = z % 2
    match = zpar == yh
    pair = b // 2
    bset = b % 2

    def dev(dp_, tn_):
        return {"dp": dp_, "tensor": tn_}

    def dpi(x_, yh_, c_):
        return (x_ * 2 + yh_) * 2 + c_

    pending = []
    pending_out = []
    counter = [0]

    def remote(src, dst, rsem, where, cond=None, sink=pending):
        n = counter[0]
        counter[0] += 1
        copy = pltpu.make_async_remote_copy(
            src_ref=src,
            dst_ref=dst,
            send_sem=send_sem.at[n],
            recv_sem=rsem,
            device_id=where,
            device_id_type=MESH,
        )
        if cond is None:
            copy.start()
        else:
            pl.when(cond)(copy.start)
        sink.append((cond, copy))

    def sent(sink, count=None):
        done = sink[:count]
        del sink[:count]
        for cond, copy in done:
            if cond is None:
                copy.wait_send()
            else:
                pl.when(cond)(copy.wait_send)

    def local(src, dst, sem, cond=None):
        copy = pltpu.make_async_copy(src, dst, sem)
        if cond is None:
            copy.start()
        else:
            pl.when(cond)(copy.start)

    def arrived(dst, sem):
        pltpu.make_async_copy(dst, dst, sem).wait()

    def to(src, dst, rsem, dp_, tn_):
        here = jnp.logical_and(dp_ == dp, tn_ == tn)
        remote(src, dst, rsem, dev(dp_, tn_), jnp.logical_not(here))
        local(src, dst, rsem, here)

    xr = (x + 1) % NX
    xl = (x + NX - 1) % NX
    xo = (x + 2) % NX
    zr = (z + 1) % NZ
    zl = (z + NZ - 1) % NZ
    right_z = dev(dp, zr * NB + b)
    left_z = dev(dp, zl * NB + b)

    table_copy = pltpu.make_async_copy(table_ref, tab, loc_sem.at[0])
    table_copy.start()
    local(tok_ref, tokv.at[dp], tok_sem.at[dp])
    own_shard = wbuf.at[bset, x, c]
    own_sem = w_sem.at[((bset * NX + x) * 2 + c) * 2]
    local(wq_ref, own_shard.at[pl.ds(0, 512)], own_sem)
    for h in (0, 1):
        local(
            wkv_ref.at[:, pl.ds(h * 256, 256)], own_shard.at[pl.ds(512 + h * 64, 64)], own_sem
        )

    barrier = pltpu.get_barrier_semaphore()
    partners = 0
    for i in range(1, 16):
        pl.semaphore_signal(barrier, inc=1, device_id=dev((dp + i) % 16, tn), device_id_type=MESH)
        partners += 1
    for i in range(1, 8):
        if i == 4:
            continue
        u = (yh * 4 + b + i) % 8
        pl.semaphore_signal(
            barrier, inc=1, device_id=dev(dpi(x, u // 4, c), z * NB + u % 4), device_id_type=MESH
        )
        partners += 1
    for where in (right_z, left_z):
        pl.semaphore_signal(barrier, inc=1, device_id=where, device_id_type=MESH)
        partners += 1

    pl.semaphore_wait(barrier, partners)

    for i in range(1, 16):
        e_ = (x * 2 + c + 8 - i % 8) % 8
        there = dpi(e_ // 2, (yh + i // 8) % 2, e_ % 2)
        remote(tok_ref, tokv.at[dp], tok_sem.at[dp], dev(there, tn))

    class Gather:
        def __init__(self, buf, sem, half, sink):
            self.buf, self.sem, self.half, self.sink = buf, sem, half, sink

        def slot(self, q, x_, c_, h=None):
            ref = self.buf.at[q, x_, c_]
            if h is None:
                return ref
            return ref.at[pl.ds(h * self.half, self.half)]

        def s(self, q, x_, c_, h=0):
            return self.sem.at[((q * NX + x_) * 2 + c_) * 2 + h]

        def send(self, src, q, x_, where):
            remote(src, self.slot(q, x_, c), self.s(q, x_, c), where, sink=self.sink)

        def to_pair(self):
            own = (bset, x)
            src = self.slot(*own, c)
            arrived(src, self.s(*own, c))
            self.send(src, *own, dev(dp, z * NB + pair * 2 + 1 - bset))

        def first(self):
            own = (bset, x)
            src = self.slot(*own, c)
            self.send(src, *own, dev(dpi(xr, yh, c), tn))
            self.send(src, *own, dev(dpi(xl, yh, c), tn))
            self.send(src, *own, dev(dpi(x, yh, 1 - c), tn))

        def second(self):
            q = 1 - bset
            arrived(self.slot(q, x, c), self.s(q, x, c))
            src = self.slot(q, x, c)
            self.send(src, q, x, dev(dpi(xr, yh, c), tn))
            self.send(src, q, x, dev(dpi(xl, yh, c), tn))
            self.send(src, q, x, dev(dpi(x, yh, 1 - c), tn))

        def relay(self, q):
            for x_, h, to_x in ((xl, 0, xr), (xr, 1, xl)):
                arrived(self.slot(q, x_, c), self.s(q, x_, c))
                remote(
                    self.slot(q, x_, c, h),
                    self.slot(q, x_, c, h),
                    self.s(q, x_, c, h),
                    dev(dpi(to_x, yh, c), tn),
                    sink=self.sink,
                )
                self.send(self.slot(q, x_, c), q, x_, dev(dpi(x, yh, 1 - c), tn))

        def last(self, q):
            for h in (0, 1):
                arrived(self.slot(q, xo, c, h), self.s(q, xo, c, h))
            self.send(self.slot(q, xo, c), q, xo, dev(dpi(x, yh, 1 - c), tn))

        def finish(self):
            for q in (0, 1):
                for x_ in range(NX):
                    arrived(self.slot(q, x_, 1 - c), self.s(q, x_, 1 - c))

    wqkv = Gather(wbuf, w_sem, 320, pending)
    wout = Gather(wobuf, wo_sem, 128, pending_out)
    wqkv.to_pair()
    wqkv.first()
    local(wo_ref, wout.slot(bset, x, c), wout.s(bset, x, c))

    place = x * 2 + c

    def source(i):
        e = (place + i % 8) % 8
        s = (yh + i // 8) % 2
        return e, s, dpi(e // 2, s, e % 2)

    def to_scalar(i):
        _, _, d2 = source(i)
        return pltpu.make_async_copy(tokv.at[d2], toks.at[d2], loc_sem.at[1 + i % 2])

    def fetch(i):
        _, _, d2 = source(i)
        arrived(tokv.at[d2], tok_sem.at[d2])
        to_scalar(i).start()

    fetch(0)
    table_copy.wait()

    lane = lax.broadcasted_iota(jnp.int32, (16, 128), 1)
    wide = lax.broadcasted_iota(jnp.int32, (16, 256), 1)
    feature = lax.broadcasted_iota(jnp.int32, (16, 256), 0)
    gain_column = jnp.sum(
        jnp.where(wide == dp * 16 + feature, gain_ref[...].astype(F32)[None], 0.0),
        axis=1,
        keepdims=True,
    )
    gain_tail = jnp.where(lane == NROWS - 128, gain_column, 0.0)
    lookup_base = counter[0]
    counter[0] += 16

    def lookup_copy(e, s):
        dp2 = dpi(e // 2, zpar, e % 2)
        return dp2, pltpu.make_async_remote_copy(
            src_ref=lsend.at[e, s],
            dst_ref=lrecv.at[dp, s],
            send_sem=send_sem.at[lookup_base + e * 2 + s],
            recv_sem=l_sem,
            device_id=dev(dp2, tn),
            device_id_type=MESH,
        )

    def lookup(i, carry):
        e, s, d2 = source(i)
        pl.when(i < 15)(lambda: fetch(i + 1))
        to_scalar(i).wait()
        for half, count in ((0, 128), (1, NROWS - 128)):
            found = jnp.zeros((16, 128), F32) if half == 0 else gain_tail
            for n in range(count):
                row = half * 128 + n
                token = toks[d2, row % 4, row // 4]
                block = lax.shift_right_logical(token, 7)
                tile = tab[:, pl.ds(block * 128, 128)].astype(F32)
                picked = jnp.where(lane == jnp.bitwise_and(token, 127), tile, 0.0)
                found = jnp.where(lane == n, jnp.sum(picked, axis=1, keepdims=True), found)
            lsend[e, s, :, pl.ds(half * 128, 128)] = found.astype(BF)

        dp2, copy = lookup_copy(e, s)
        pl.when(dp2 != dp)(copy.start)
        pl.when(dp2 == dp)(pltpu.make_async_copy(lsend.at[e, s], lrecv.at[dp, s], l_sem).start)
        return carry

    lax.fori_loop(0, 16, lookup, 0)
    wqkv.second()
    wqkv.relay(bset)

    k_here = z // 2

    pl.when(match)(lambda: arrived(lrecv, l_sem))
    for s in (0, 1):

        @pl.when(match)
        def _(s=s):
            features = lrecv[:, s].reshape(256, 256).astype(F32)
            xt[s] = features.T[:XROWS].astype(BF)

        for h in (0, 1):
            b2 = (1 - pair if h == 0 else pair) * 2 + s
            here = b2 == b
            dst = xb.at[k_here, b]
            sem = x_sem.at[k_here * NB + b]
            remote(
                xt.at[s],
                dst,
                sem,
                dev(dp, z * NB + b2),
                jnp.logical_and(match, jnp.logical_not(here)),
            )
            local(xt.at[s], dst, sem, jnp.logical_and(match, here))

    def by_b(values):
        return jnp.where(
            b == 0, values[0], jnp.where(b == 1, values[1], jnp.where(b == 2, values[2], values[3]))
        )

    nearest = [by_b(v) for v in ((0, 1, 2, 3), (1, 0, 3, 2), (2, 2, 1, 1), (3, 3, 0, 0))]
    if_match = [(0, i) for i in range(4)]
    if_match += [(d, i) for i in range(4) for d in (2, 6)]
    if_match += [(4, i) for i in range(4)]
    if_not = [(d, i) for i in range(4) for d in (1, 7)]
    if_not += [(d, i) for i in range(4) for d in (3, 5)]
    blocks = []
    for (d_m, i_m), (d_n, i_n) in zip(if_match, if_not):
        delta = jnp.where(match, d_m, d_n)
        b_ = jnp.where(match, nearest[i_m], nearest[i_n])
        blocks.append((delta, ((z - delta + NZ) % NZ) // 2, b_))

    row40 = lax.broadcasted_iota(jnp.int32, (QROWS, 128), 0)
    lane40 = lax.broadcasted_iota(jnp.int32, (QROWS, 128), 1)

    def angles():
        lengths = len_ref[...].astype(F32)
        row_of = lax.broadcasted_iota(jnp.int32, (QROWS, 40), 0) // 4 + b * 10
        all_rows = lax.broadcasted_iota(jnp.int32, (QROWS, 40), 1)
        length = jnp.sum(jnp.where(all_rows == row_of, lengths, 0.0), axis=1, keepdims=True)
        turn = (length + (row40 % 4).astype(F32)) * freq_ref[...]
        cos_ref[...] = jnp.cos(turn)
        sin_ref[...] = jnp.where(lane40 < HEAD // 2, -1.0, 1.0) * jnp.sin(turn)
        return length

    def forward(n):
        delta, k, b_ = blocks[n]
        reach = jnp.where(b_ < 2, 4, 3)
        block = xb.at[k, b_]
        sem = x_sem.at[k * NB + b_]
        arrived(block, sem)
        if n < 4:
            onward = delta == 0
        else:
            onward = False
        onward = jnp.logical_or(
            onward, jnp.logical_and(delta > reach, 8 - delta < 7 - reach)
        )
        remote(block, block, sem, right_z, delta < reach)
        remote(block, block, sem, left_z, onward)

    def project(n):
        _, k, b_ = blocks[n]
        c_ = b_ // 2
        h = b_ % 2
        raw = xb[k, b_].astype(F32)
        rows = raw[:NROWS]
        gain = raw[NROWS : NROWS + 1]
        scaled = (rows * gain).astype(BF)
        square = rows * rows
        square = square[:, :128] + square[:, 128:]
        parts = [
            jnp.dot(scaled, wbuf[q, k, c_, pl.ds(h * 256, 256)], preferred_element_type=F32)
            for q in (0, 1)
        ]
        keyval = jnp.concatenate(
            [wbuf[q, k, c_, pl.ds(512 + h * 64, 64)] for q in (0, 1)], axis=0
        )
        kv = lax.dot_general(
            scaled, keyval, (((1,), (1,)), ((), ())), preferred_element_type=F32
        )
        if n == 0:
            ssq[...] = square
            qacc[:, :256] = parts[0]
            qacc[:, 256:] = parts[1]
            kvacc[...] = kv
        else:
            ssq[...] += square
            qacc[:, :256] += parts[0]
            qacc[:, 256:] += parts[1]
            kvacc[...] += kv

    forward(0)
    wqkv.relay(1 - bset)
    forward(1)
    wqkv.last(bset)
    forward(2)
    forward(3)
    wout.to_pair()
    wqkv.last(1 - bset)
    for n in range(4, 16):
        forward(n)
        if n == 5:
            wout.first()
        if n == 8:
            for i in range(NB):
                b2 = (b + i) % NB
                to(cache_ref.at[pl.ds(b2 * 10, 10)], cbuf.at[b], c_sem, dp, z * NB + b2)
        if n == 9:
            wout.second()
        if n == 11:
            wqkv.finish()
            for m in range(11):
                project(m)
        if n >= 11:
            project(n)
        if n == 14:
            wout.relay(bset)

    before_q = len(pending)

    diagonal = row40 == lane40
    row8 = lax.broadcasted_iota(jnp.int32, (8, 128), 0)
    for i in range(NB):
        total = jnp.sum(ssq[i * QROWS : (i + 1) * QROWS], axis=1, keepdims=True)
        flat = jnp.sum(jnp.where(diagonal, total, 0.0), axis=0, keepdims=True)
        high = flat.astype(BF).astype(F32)
        low = flat - high
        tail = jnp.where(row8 == 0, high, jnp.where(row8 == 1, low, 0.0))
        tail = jnp.concatenate([tail, jnp.zeros((8, 512), F32)], axis=1)
        body_rows = jnp.concatenate(
            [qacc[i * QROWS : (i + 1) * QROWS], kvacc[i * QROWS : (i + 1) * QROWS]], axis=1
        )
        qsend[i] = jnp.concatenate([body_rows, tail], axis=0).astype(BF)
        to(
            qsend.at[i],
            qrecv.at[yh, pair],
            q_sem.at[yh * 2 + pair],
            dpi(x, bset, c),
            z * NB + i,
        )

    wout.relay(1 - bset)

    length = angles()
    col = lax.broadcasted_iota(jnp.int32, (QROWS, 640), 1)
    row = lax.broadcasted_iota(jnp.int32, (QROWS, 640), 0) // 4
    within = col % 160
    position = (col // 160) * 16 + within % 16
    old_ok = jnp.logical_and(within // 16 == row, position.astype(F32) < length)
    new_ok = jnp.logical_and(
        lane40 // 4 == row40 // 4, jnp.logical_and(lane40 <= row40, lane40 < QROWS)
    )
    old_bias = jnp.where(old_ok, 0.0, -1e30)
    new_bias = jnp.where(new_ok, 0.0, -1e30)
    old_bias = jnp.concatenate([old_bias] * 8, axis=0)
    new_bias = jnp.concatenate([new_bias] * 8, axis=0)
    sent(pending, before_q)

    def lookup_sent(i, carry):
        dp2, copy = lookup_copy(i // 2, i % 2)
        pl.when(dp2 != dp)(copy.wait_send)
        return carry

    lax.fori_loop(0, 16, lookup_sent, 0)

    for i in range(NB):
        arrived(qrecv.at[i // 2, i % 2], q_sem.at[i])
    arrived(cbuf, c_sem)

    tails = qrecv[0, 0, 32:QPAD, :128].astype(F32) + qrecv[1, 0, 32:QPAD, :128].astype(F32)
    flat = tails[8:9] + tails[9:10]
    total = jnp.sum(jnp.where(diagonal, flat, 0.0), axis=1, keepdims=True)
    factor = lax.rsqrt(total * (1.0 / FULL) + EPS)
    cosine = cos_ref[...]
    sine = sin_ref[...]

    def rope(u):
        return u * cosine + pltpu.roll(u, HEAD // 2, 1) * sine

    heads = []
    news = []
    for p in (0, 1):
        both = qrecv[0, p].astype(F32) + qrecv[1, p].astype(F32)
        both = both[:QROWS] * factor
        for i in range(4):
            heads.append(rope(both[:, i * HEAD : (i + 1) * HEAD]))
        news.append(both[:, 512:640])
    query = jnp.concatenate(heads, axis=0).astype(BF)
    no_rows = jnp.zeros((128 - QROWS, HEAD), F32)
    key_new = rope(news[0].astype(BF).astype(F32))
    key_new = jnp.concatenate([key_new, no_rows], axis=0).astype(BF)
    value_new = jnp.concatenate([news[1], no_rows], axis=0).astype(BF)
    keys = cbuf[:, :, :, :HEAD].reshape(640, HEAD)
    values = cbuf[:, :, :, HEAD:].reshape(640, HEAD)

    contract_last = (((1,), (1,)), ((), ()))
    inv_root = 1.0 / math.sqrt(HEAD)
    scores_old = lax.dot_general(query, keys, contract_last, preferred_element_type=F32) * inv_root
    scores_new = (
        lax.dot_general(query, key_new, contract_last, preferred_element_type=F32) * inv_root
    )
    scores_old = jnp.where(old_bias == 0.0, scores_old, -1e30)
    scores_new = jnp.where(new_bias == 0.0, scores_new, -1e30)
    top = jnp.maximum(
        jnp.max(scores_old, axis=1, keepdims=True), jnp.max(scores_new, axis=1, keepdims=True)
    )
    exp_old = jnp.exp(scores_old - top)
    exp_new = jnp.exp(scores_new - top)
    totals = jnp.sum(exp_old, axis=1, keepdims=True) + jnp.sum(exp_new, axis=1, keepdims=True)
    share = 1.0 / totals
    probs_old = (exp_old * share).astype(BF)
    probs_new = (exp_new * share).astype(BF)
    attended = jnp.dot(probs_old, values, preferred_element_type=F32)
    attended = attended + jnp.dot(probs_new, value_new, preferred_element_type=F32)
    for p in (0, 1):
        side = jnp.concatenate(
            [attended[(4 * p + i) * QROWS : (4 * p + i + 1) * QROWS] for i in range(4)], axis=1
        )
        asend[p] = jnp.concatenate([side, jnp.zeros((QPAD - QROWS, 512), F32)], axis=0).astype(BF)
        for y_ in (0, 1):
            to(asend.at[p], arecv.at[b], a_sem.at[b], dpi(x, y_, c), z * NB + p * 2 + yh)

    wout.last(bset)
    wout.last(1 - bset)
    wout.finish()
    sent(pending_out)
    for i in range(NB):
        arrived(arecv.at[i], a_sem.at[i])
    att[...] = jnp.concatenate(
        [arecv[i].astype(F32)[:QROWS] for i in range(NB)], axis=0
    ).astype(BF)

    cross = ((2, 0), (3, 1), (0, 2), (1, 3))
    if_match = [(4, i) for i in range(4)]
    if_match += [item for i, j in cross for item in ((2, i), (6, j))]
    if_match += [(0, i) for i in (2, 0, 3, 1)]
    if_not = [item for i, j in cross for item in ((3, i), (5, j))]
    if_not += [item for i, j in cross for item in ((1, i), (7, j))]
    for n in range(16):
        (d_m, i_m), (d_n, i_n) = if_match[n], if_not[n]
        delta = jnp.where(match, d_m, d_n)
        b_ = jnp.where(match, i_m, i_n)
        k = ((z + delta) % NZ) // 2
        reach = jnp.where(b_ < 2, 4, 3)
        is_end = delta == 0
        c_ = b_ // 2
        h = b_ % 2
        part = jnp.dot(
            att[:, :256], wobuf[0, k, c_, :, pl.ds(h * 256, 256)], preferred_element_type=F32
        )
        acc[...] = part + jnp.dot(
            att[:, 256:], wobuf[1, k, c_, :, pl.ds(h * 256, 256)], preferred_element_type=F32
        )
        from_left = delta + 1 <= reach
        from_right = jnp.logical_or(delta > reach + 1, is_end)
        index = k * NB + b_

        @pl.when(from_left)
        def _(index=index, k=k, b_=b_):
            arrived(rright.at[k, b_], rr_sem.at[index])
            acc[...] += rright[k, b_].astype(F32)

        @pl.when(from_right)
        def _(index=index, k=k, b_=b_):
            arrived(rleft.at[k, b_], rl_sem.at[index])
            acc[...] += rleft[k, b_].astype(F32)

        if n == 12:
            before_end = len(pending)
        if n >= 12:

            @pl.when(jnp.logical_and(is_end, pair == 0))
            def _(k=k, b_=b_):
                acc[...] += xb[k, b_, :NROWS].astype(F32)

        src = sbuf.at[k, b_]
        src[...] = acc[...].astype(BF)
        remote(
            src,
            rright.at[k, b_],
            rr_sem.at[index],
            right_z,
            jnp.logical_and(delta >= 1, delta <= reach),
        )
        remote(src, rleft.at[k, b_], rl_sem.at[index], left_z, delta > reach)
        if n >= 12:
            dp_ = dpi(x, bset, c)
            tn_ = z * NB + b_
            here = jnp.logical_and(dp_ == dp, tn_ == tn)
            remote(
                src,
                frecv.at[pair],
                f_sem.at[pair],
                dev(dp_, tn_),
                jnp.logical_and(is_end, jnp.logical_not(here)),
            )
            local(src, frecv.at[pair], f_sem.at[pair], jnp.logical_and(is_end, here))

    sent(pending, before_end)
    for p in (0, 1):
        arrived(frecv.at[p], f_sem.at[p])
    hidden = frecv[0].astype(F32) + frecv[1].astype(F32)
    hidden = jnp.concatenate([hidden, jnp.zeros((256 - NROWS, 256), F32)], axis=0).astype(BF)
    to_row = lax.broadcasted_iota(jnp.int32, (NROWS, 256), 0)
    from_row = lax.broadcasted_iota(jnp.int32, (NROWS, 256), 1)
    order = jnp.where(from_row == (to_row % 40) * 4 + to_row // 40, 1.0, 0.0).astype(BF)
    out_ref[...] = jnp.dot(order, hidden, preferred_element_type=F32).astype(BF)

    sent(pending)


def body(
    token_ids, lengths, embed_table, norm_gain, w_query, key_value_weight, w_out, key_value_cache
):
    table = embed_table.reshape(16, -1)
    frequency = THETA ** (-(np.arange(64) / 64))
    frequency = jnp.asarray(np.concatenate([frequency, frequency])[None], F32)
    keyval = key_value_weight.T
    cache = key_value_cache.reshape(40, 16, 256)

    vmem = pl.BlockSpec(memory_space=pltpu.VMEM)
    anywhere = pl.BlockSpec(memory_space=pl.ANY)
    dma = pltpu.SemaphoreType.DMA
    out = pl.pallas_call(
        kernel,
        out_shape=jax.ShapeDtypeStruct((NROWS, 256), BF),
        in_specs=[vmem, vmem, anywhere, vmem, vmem, anywhere, anywhere, anywhere, anywhere],
        out_specs=vmem,
        scratch_shapes=[
            pltpu.VMEM((16, 81920), BF),
            pltpu.VMEM((16, 4, 40), jnp.int32),
            pltpu.SMEM((16, 4, 40), jnp.int32),
            pltpu.VMEM((8, 2, 16, 256), BF),
            pltpu.VMEM((QROWS, HEAD), F32),
            pltpu.VMEM((QROWS, HEAD), F32),
            pltpu.VMEM((16, 2, 16, 256), BF),
            pltpu.VMEM((2, XROWS, 256), BF),
            pltpu.VMEM((4, NB, XROWS, 256), BF),
            pltpu.VMEM((2, NX, 2, 640, 256), BF),
            pltpu.VMEM((2, NX, 2, 256, 512), BF),
            pltpu.VMEM((NB, 10, 16, 256), BF),
            pltpu.VMEM((NB, QPAD, 640), BF),
            pltpu.VMEM((2, 2, QPAD, 640), BF),
            pltpu.VMEM((2, QPAD, 512), BF),
            pltpu.VMEM((NB, QPAD, 512), BF),
            pltpu.VMEM((NROWS, 512), BF),
            pltpu.VMEM((NROWS, 512), F32),
            pltpu.VMEM((NROWS, 128), F32),
            pltpu.VMEM((NROWS, 128), F32),
            pltpu.VMEM((NROWS, 256), F32),
            pltpu.VMEM((4, NB, NROWS, 256), BF),
            pltpu.VMEM((4, NB, NROWS, 256), BF),
            pltpu.VMEM((4, NB, NROWS, 256), BF),
            pltpu.VMEM((2, NROWS, 256), BF),
            dma((192,)),
            dma((3,)),
            dma((16,)),
            dma,
            dma((16,)),
            dma((32,)),
            dma((32,)),
            dma,
            dma((4,)),
            dma((4,)),
            dma((16,)),
            dma((16,)),
            dma((2,)),
        ],
        compiler_params=pltpu.CompilerParams(
            collective_id=0, has_side_effects=True, vmem_limit_bytes=56 * 1024 * 1024
        ),
        name="decode_block",
    )(token_ids, lengths[None], table, norm_gain, frequency, w_query, keyval, w_out, cache)
    return out.reshape(4, 40, 256)


def solution(mesh):
    in_specs = (
        P(None, "dp"),
        P("dp"),
        P(None, "tensor", "dp", None),
        P("tensor"),
        P("dp", "tensor"),
        P("dp", "tensor"),
        P("tensor", "dp"),
        P("dp", "tensor", None, None),
    )
    out_specs = P(None, "dp", "tensor")
    return jax.shard_map(body, mesh=mesh, in_specs=in_specs, out_specs=out_specs, check_vma=False)
```
